512 devices in a mesh: space: 128 (over y, z, core), chan: 4 (over x).
Axes of the slice: x: 4, y: 4, z: 16, core: 2. Of those that a mesh axis runs over, the one named last changes fastest.
Arguments:
- features: float32 [16384, 512], P('space', 'chan'), may hold values from -6 to 6
- weights: float32 [27, 512, 512], P(None, 'space', 'chan'), may hold values from -0.0546875 to 0.0546875
- cotangent: float32 [16384, 512], P('space', 'chan'), may hold values from -6 to 6
- rule_src: int32 [3456, 128], P('space'), may hold values from 0 to 383
- rule_dst: int32 [3456, 128], P('space'), may hold values from 0 to 127, as said below
- block_count: int32 [3456], P('space'), may hold values from 32 to 128, as said below
- send_rows: int32 [16384, 2], P('space'), may hold values from 0 to 127
Outputs:
- conv_out: float32 [16384, 512], P('space', 'chan')
- grad_features: float32 [16384, 512], P('space', 'chan')
The draws below stay inside these ranges and needn't reach their ends.
Inputs may be any that keep to these rules, and one draw needn't show every extreme that they name: `rule_dst`: for every device and offset, the 1 block hold each of the device's local voxel indices exactly once. `block_count`: every device has at least one full block; rows at or past the count are padding whose indices must be ignored.
All inputs are finite; a program needn't handle non-finite values.
Results may differ from the reference program's by a relative error of at most 0.0003.
Values sent between devices are 32-bit elements; how exact they have to be, the bound alone decides.
No kernel may reach another device: no remote copies, remote signals or barrier semaphores. Data moves between devices by JAX's collectives and lax.ppermute only.
A program may use at most 64 MiB of HBM per device.

```python
import jax
import jax.numpy as jnp
from jax import lax

C = 512
OFFSETS = 27
BLOCK = 128
VOX_DEV = 128
HALO_PEER = 2
BLOCKS_OFF = 1
EXTENDED = 384
VOXELS = 16384
N_SPACE = 128


def draw_rule_dst(key, part):
    key = jax.random.fold_in(key, 11)
    row_keys = jax.random.split(key, N_SPACE * OFFSETS)
    orders = jax.vmap(lambda subkey: jax.random.permutation(subkey, VOX_DEV))(row_keys)
    return orders.astype(jnp.int32).reshape(N_SPACE * OFFSETS * BLOCKS_OFF, BLOCK)


def draw_block_count(key, part):
    key = jax.random.fold_in(key, 23)
    key_level, key_count, key_full = jax.random.split(key, 3)
    blocks = OFFSETS * BLOCKS_OFF
    ceiling = jax.random.randint(key_level, (N_SPACE, 1), 2, 5) * (BLOCK // 4)
    drawn = jax.random.randint(key_count, (N_SPACE, blocks), BLOCK // 4, BLOCK + 1)
    counts = jnp.minimum(drawn, ceiling)
    chosen = jax.random.randint(key_full, (N_SPACE, 1), 0, blocks)
    counts = jnp.where(jnp.arange(blocks)[None, :] == chosen, BLOCK, counts)
    return counts.reshape(-1).astype(jnp.int32)


def plant(result, own_key, low, top_value):
    spot = [jax.random.randint(jax.random.fold_in(own_key, axis), (), 0, length) for axis, length in enumerate(result.shape)]
    main_axis = result.shape.index(max(result.shape))
    beside = spot[:main_axis] + [(spot[main_axis] + 1) % result.shape[main_axis]] + spot[main_axis + 1:]
    return result.at[tuple(spot)].set(low).at[tuple(beside)].set(top_value)


def levels(rng, extent, cuts, low, high):
    factor_of = 1.0
    for axis_at, parts in cuts:
        steps = jax.random.uniform(jax.random.fold_in(jax.random.fold_in(rng, 6), axis_at), (parts,), jnp.float32, low / len(cuts), high / len(cuts))
        factor_of = factor_of * jnp.repeat(jnp.exp(steps), extent[axis_at] // parts).reshape((-1,) + (1,) * (len(extent) - 1 - axis_at))
    return factor_of


def normal_values(stream_key, dims, scale, most, shards=(), kind=jnp.bfloat16):
    values = scale * jax.random.normal(stream_key, dims, jnp.float32)
    if shards:
        values = values * levels(stream_key, dims, shards, -0.22, 0.18)
    return jnp.clip(values, -most, most).astype(kind)


def setup_inputs(seed: int = 0) -> dict:
    seeds = jax.random.split(jax.random.key(seed), 8)
    return {
        "features": normal_values(seeds[0], (VOXELS, C), 1.0, 6.0, ((0, 128), (1, 4)), jnp.float32),
        "weights": normal_values(seeds[1], (OFFSETS, C, C), (OFFSETS * C) ** -0.5, 0.0546875, ((1, 128), (2, 4)), jnp.float32),
        "cotangent": normal_values(seeds[2], (VOXELS, C), 1.0, 6.0, ((0, 128), (1, 4)), jnp.float32),
        "rule_src": plant(jax.random.randint(seeds[3], (N_SPACE * OFFSETS * BLOCKS_OFF, BLOCK), 0, EXTENDED), jax.random.fold_in(seeds[3], 1), 0, EXTENDED - 1).astype(jnp.int32),
        "rule_dst": draw_rule_dst(jax.random.fold_in(seeds[7], 71), 0),
        "block_count": draw_block_count(jax.random.fold_in(seeds[7], 71), 0),
        "send_rows": plant(jax.random.randint(seeds[6], (N_SPACE * N_SPACE, HALO_PEER), 0, VOX_DEV), jax.random.fold_in(seeds[6], 1), 0, VOX_DEV - 1).astype(jnp.int32),
    }


def reference(features, weights, cotangent, rule_src, rule_dst, block_count, send_rows):
    peer_count = N_SPACE
    full_width = C
    pair_slots = BLOCKS_OFF * BLOCK
    sources_all = rule_src.reshape(peer_count, OFFSETS, pair_slots)
    targets_all = rule_dst.reshape(peer_count, OFFSETS, pair_slots)
    live_all = (jnp.arange(BLOCK, dtype=jnp.int32)[None, :] < block_count[:, None]).astype(jnp.float32)
    live_all = live_all.reshape(peer_count, OFFSETS, pair_slots)
    send_table = send_rows.reshape(peer_count, peer_count, HALO_PEER)
    owner_base = (jnp.arange(peer_count, dtype=jnp.int32) * VOX_DEV)[:, None]

    def one_device(device):
        start = (device * VOX_DEV).astype(jnp.int32)
        local_rows = lax.dynamic_slice_in_dim(features, start, VOX_DEV, 0)
        local_grad = lax.dynamic_slice_in_dim(cotangent, start, VOX_DEV, 0)
        incoming = (send_table[:, device, :] + owner_base).reshape(-1)
        extended = jnp.concatenate([local_rows, features[incoming]], 0)

        def forward_step(running, offset):
            picked = extended[sources_all[device, offset]]
            product = jnp.dot(picked, weights[offset], precision=lax.Precision.HIGHEST, preferred_element_type=jnp.float32)
            product = product * live_all[device, offset][:, None]
            return running.at[targets_all[device, offset]].add(product), None

        output_rows, _ = lax.scan(forward_step, jnp.zeros((VOX_DEV, full_width), jnp.float32), jnp.arange(OFFSETS, dtype=jnp.int32))

        def backward_step(running, offset):
            picked = local_grad[targets_all[device, offset]]
            product = jnp.dot(picked, weights[offset].T, precision=lax.Precision.HIGHEST, preferred_element_type=jnp.float32)
            product = product * live_all[device, offset][:, None]
            return running.at[sources_all[device, offset]].add(product), None

        grad_ext, _ = lax.scan(backward_step, jnp.zeros((VOX_DEV + peer_count * HALO_PEER, full_width), jnp.float32), jnp.arange(OFFSETS, dtype=jnp.int32))
        return output_rows, grad_ext

    output_rows, grad_ext = lax.map(one_device, jnp.arange(peer_count, dtype=jnp.int32))
    conv_out = output_rows.reshape(-1, full_width)
    grad_flat = grad_ext[:, :VOX_DEV].reshape(-1, full_width)
    halo_part = grad_ext[:, VOX_DEV:].reshape(peer_count, peer_count, HALO_PEER, full_width)
    destinations = jnp.transpose(send_table, (1, 0, 2)) + owner_base[None]
    grad_features = grad_flat.at[destinations.reshape(-1)].add(halo_part.reshape(-1, full_width))
    return conv_out, grad_features
```

```python
import jax
import jax.numpy as jnp
from jax import lax
from jax.experimental import pallas as pl
from jax.experimental.pallas import tpu as pltpu
from jax.sharding import PartitionSpec as P

F32 = jnp.float32
BF16 = jnp.bfloat16
NY = 4
CORES = 2
CHUNKS = 3
SMALL, LARGE = 16, 63


def iota(shape, dim):
    return lax.broadcasted_iota(jnp.int32, shape, dim)


def split2(x):
    high = x.astype(BF16)
    return high, (x - high.astype(F32)).astype(BF16)


def split3(x):
    high = x.astype(BF16)
    rest = x - high.astype(F32)
    middle = rest.astype(BF16)
    return high, middle, (rest - middle.astype(F32)).astype(BF16)


def dot(a, b):
    return jnp.dot(a, b, preferred_element_type=F32)


def as_onehot(mask):
    return jnp.where(mask, 1.0, 0.0).astype(BF16)


def pick_left(onehot, x):
    a, b, c = split3(x)
    return (dot(onehot, a) + dot(onehot, b)) + dot(onehot, c)


def pick_right(x, onehot):
    a, b, c = split3(x)
    return (dot(a, onehot) + dot(b, onehot)) + dot(c, onehot)


def to_inner(n):
    row = iota((n, n), 0)
    place = ((row >> 2) & 1) * 64 + (row >> 3) * 4 + (row & 3)
    return as_onehot(iota((n, n), 1) == place)


def from_inner(n):
    row = iota((n, n), 0)
    place = ((row >> 2) & 15) * 8 + (row >> 6) * 4 + (row & 3)
    return as_onehot(iota((n, n), 1) == place)


FEATURES, SOURCES, TARGETS, SENDS, SHARED = 128, 256, 288, 320, 328


def onehot_rows(line, rows):
    return as_onehot(line.astype(jnp.int32) == iota((rows, line.shape[1]), 0))


def started(pairs, sems):
    copies = [pltpu.make_async_copy(a, b, sems.at[i]) for i, (a, b) in enumerate(pairs)]
    for copy in copies:
        copy.start()
    return copies


def prepare_kernel(
    count_ref, features_in, cot_in, send_in, src_in, dst_in, shared_ref,
    features_ref, send_ref, src_ref, dst_ref, sems,
):
    rows, width = features_ref.shape
    offsets, block = src_ref.shape
    copies = started(
        [
            (features_in, features_ref),
            (send_in, send_ref),
            (src_in, src_ref),
            (dst_in, dst_ref),
            (cot_in, shared_ref.at[pl.ds(0, rows)]),
        ],
        sems,
    )
    for copy in copies:
        copy.wait()
    shared_ref[FEATURES : FEATURES + rows, :] = pick_right(features_ref[...], to_inner(width))
    shared_ref[SOURCES:SHARED, :] = jnp.zeros((SHARED - SOURCES, width), F32)
    for k in range(offsets):
        live = iota((1, block), 1) < count_ref[k]
        shared_ref[SOURCES + k : SOURCES + k + 1, :] = jnp.where(live, src_ref[k : k + 1, :], -1).astype(F32)
    shared_ref[TARGETS : TARGETS + offsets, :] = dst_ref[...].astype(F32)
    shared_ref[SENDS : SENDS + send_ref.shape[0], :] = send_ref[...].astype(F32)


def outgoing_kernel(core_ref, shared_ref, outgoing_ref, cot_ref, sends_ref, picked_ref):
    rows, width = picked_ref.shape
    half = width // CORES
    slots = sends_ref.shape[0] // CORES
    chips = picked_ref.shape[0] // CORES
    for device in range(CORES):
        base = device * SHARED
        cot_ref[device * rows : (device + 1) * rows, :] = shared_ref[base : base + rows, :]
        inner = shared_ref[base + FEATURES : base + FEATURES + rows, :]
        parts = split3(pltpu.roll(inner, half * core_ref[0], axis=1))
        for slot in range(slots):
            line = shared_ref[base + SENDS + slot : base + SENDS + slot + 1, :]
            sends_ref[device * slots + slot : device * slots + slot + 1, :] = line
            onehot = onehot_rows(line, rows)
            a, b, c = (
                lax.dot_general(onehot, part, (((0,), (0,)), ((), ())), preferred_element_type=F32)
                for part in parts
            )
            picked_ref[...] = (a + b) + c
            both = [picked_ref[pl.ds(d, chips, stride=CORES), :][:, :half] for d in range(CORES)]
            outgoing_ref[pl.ds(device * slots + slot, chips, stride=CORES * slots), :] = jnp.concatenate(
                both, axis=1
            )


def regroup_kernel(gathered_ref, grouped_ref):
    offsets, inner, _ = grouped_ref.shape
    depth = gathered_ref.shape[1]
    for k in range(offsets):
        for z in range(inner // depth):
            grouped_ref[k, z * depth : (z + 1) * depth, :] = gathered_ref[z * offsets + k]


def pairs_of(shared_ref, device, k, local, rows):
    start = device * SHARED + k
    src = shared_ref[start + SOURCES : start + SOURCES + 1, :]
    dst = shared_ref[start + TARGETS : start + TARGETS + 1, :]
    mine = dst == iota((local, dst.shape[1]), 0).astype(F32)
    source = jnp.sum(jnp.where(mine, src + 1.0, 0.0), axis=1, keepdims=True)
    return as_onehot(iota((local, rows), 1) == source.astype(jnp.int32) - 1)


def kernel_rows(pieces):
    wide = jnp.concatenate(pieces, axis=2)
    return wide.reshape(wide.shape[0] * wide.shape[1], wide.shape[2])


def core_kernel(order_ref, *refs):
    shared_in, incoming_in = refs[:2]
    cot_in = refs[2 : NY + 2]
    piece_in = refs[NY + 2 : 2 * NY + 2]
    refs = refs[2 * NY + 2 :]
    halo_out, local_ref, other_ref, *part_outs = refs[: NY + 3]
    shared_ref, incoming_ref, cot_ref, pieces_ref, turned_ref, table_ref, total_ref, halo_ref = refs[
        NY + 3 : -4
    ]
    first_sems, cot_sems, piece_sems, out_sems = refs[-4:]
    rows, width = part_outs[0].shape
    both_rows = CORES * rows
    table_rows = table_ref.shape[0]
    offsets = pieces_ref.shape[1]
    half = pieces_ref.shape[2]
    step = offsets // CHUNKS
    core = order_ref[NY]

    def piece_copy(chunk, n):
        span = pl.ds(chunk * step, step)
        return pltpu.make_async_copy(piece_in[n].at[span], pieces_ref.at[n, span], piece_sems.at[chunk, n])

    first = [
        pltpu.make_async_copy(shared_in, shared_ref, first_sems.at[0]),
        pltpu.make_async_copy(incoming_in, incoming_ref, first_sems.at[1]),
    ]
    cots = [
        pltpu.make_async_copy(cot_in[m], cot_ref.at[m], cot_sems.at[m])
        for m in range(NY)
    ]
    for copy in first + cots:
        copy.start()
    for chunk in range(CHUNKS):
        for n in range(NY):
            piece_copy(chunk, n).start()
    for copy in first + cots:
        copy.wait()
    for n in range(NY):
        high, low = split2(cot_ref[order_ref[NY + 1 + n]].T)
        turned_ref[n * width : (n + 1) * width, :both_rows] = high
        turned_ref[n * width : (n + 1) * width, both_rows:] = low
    local = [
        pltpu.roll(
            shared_ref[d * SHARED + FEATURES : d * SHARED + FEATURES + rows, :], half * core, axis=1
        )[:, :half]
        for d in range(CORES)
    ]
    table = jnp.concatenate([jnp.concatenate(local, axis=1), incoming_ref[...]], axis=0)
    high, low = split2(table)
    table_ref[:, :width] = high
    table_ref[:, width:] = low

    grads = [None] * CORES
    total = None
    for chunk in range(CHUNKS):
        pairs = [
            jnp.concatenate(
                [pairs_of(shared_ref, d, chunk * step + k, rows, table_rows) for k in range(step)], axis=0
            )
            for d in range(CORES)
        ]
        picked = []
        for device in range(CORES):
            both = dot(pairs[device], table_ref[...]).astype(BF16)
            for start in (device * half, width + device * half):
                picked.append(
                    jnp.concatenate(
                        [both[k * rows : (k + 1) * rows, start : start + half] for k in range(step)],
                        axis=1,
                    )
                )
        highs = jnp.concatenate([picked[0], picked[2]], axis=0)
        lows = jnp.concatenate([picked[1], picked[3]], axis=0)
        for n in range(NY):
            piece_copy(chunk, n).wait()
        span = slice(chunk * step, (chunk + 1) * step)
        high, low = split2(kernel_rows([pieces_ref[n, span] for n in range(NY)]))
        product = dot(highs, high) + dot(lows, high) + dot(highs, low)
        total = product if chunk == 0 else total + product
        wide = dot(high, turned_ref[...])
        product = wide[:, :both_rows] + wide[:, both_rows:] + dot(low, turned_ref[:, :both_rows])
        product = product.reshape(step, half, both_rows)
        for device in range(CORES):
            side = jnp.concatenate(
                [product[k][:, device * rows : (device + 1) * rows] for k in range(step)], axis=1
            )
            both = dot(jnp.concatenate(split2(side), axis=0), pairs[device])
            both = both[:half] + both[half:]
            grads[device] = both if chunk == 0 else grads[device] + both
    table = jnp.concatenate(grads, axis=0).T
    halo_ref[...] = table[rows:, :]
    outs = [pltpu.make_async_copy(halo_ref, halo_out, out_sems.at[NY])]
    outs[0].start()
    local_ref[...] = table[:rows, :]
    for n in range(NY):
        for device in range(CORES):
            part = total[device * rows : (device + 1) * rows, n * width : (n + 1) * width]
            total_ref[device, n] = part
    for s in range(NY):
        outs.append(
            pltpu.make_async_copy(
                total_ref.at[core, order_ref[2 * NY + 1 + s]], part_outs[s], out_sems.at[s]
            )
        )
        outs[-1].start()
        other_ref[s * rows : (s + 1) * rows, :] = total_ref[1 - core, order_ref[2 * NY + 1 + s]]
    for copy in outs:
        copy.wait()


def finish_kernel(core_ref, local_ref, returned_ref, sends_ref, own_ref, other_ref, grads_ref, full_ref):
    rows, width = own_ref.shape
    half = width // CORES
    slots = sends_ref.shape[0] // CORES
    chips = sends_ref.shape[1] // CORES
    spread = from_inner(width)
    spread = jnp.where(core_ref[0] == 0, spread[:half, :], spread[half:, :])
    for device in range(CORES):
        total = local_ref[:, device * half : (device + 1) * half]
        for slot in range(slots):
            line = device * slots + slot
            part = returned_ref[pl.ds(line, chips, stride=CORES * slots), :]
            for d in range(CORES):
                grads_ref[pl.ds(d, chips, stride=CORES), :half] = part[:, d * half : (d + 1) * half]
            onehot = onehot_rows(sends_ref[line : line + 1, :], rows)
            total = total + pick_left(onehot, grads_ref[:, :half])
        full_ref[device] = pick_right(total, spread)
    own_ref[...] = full_ref[core_ref[0]]
    other_ref[...] = full_ref[1 - core_ref[0]]


VMEM = pl.BlockSpec(memory_space=pltpu.VMEM)
HBM = pl.BlockSpec(memory_space=pl.ANY)
SMEM = pl.BlockSpec(memory_space=pltpu.SMEM)


def params(mebibytes):
    return pltpu.CompilerParams(vmem_limit_bytes=mebibytes * 1024 * 1024)


def whole(kernel, outs, args, in_specs=None, out_specs=None, scratch=(), mebibytes=16):
    return pl.pallas_call(
        kernel,
        out_shape=tuple(jax.ShapeDtypeStruct(s, t) for s, t in outs),
        in_specs=in_specs or [VMEM] * len(args),
        out_specs=tuple(out_specs or [VMEM] * len(outs)),
        scratch_shapes=list(scratch),
        compiler_params=params(mebibytes),
    )(*args)


def on_device(features, weights, cotangent, rule_src, rule_dst, block_count, send_rows):
    space = lax.axis_size("space")
    chan = lax.axis_size("chan")
    nz = space // (NY * CORES)
    rows, width = features.shape
    offsets = weights.shape[0]
    peers, slots = send_rows.shape
    halo_rows = peers * slots
    table_rows = rows + halo_rows
    half = width // CORES

    def place(y, z, core):
        return ((y % NY) * nz + z) * CORES + core

    where = [(y, z, core) for y in range(NY) for z in range(nz) for core in range(CORES)]
    z_groups = [[place(b, z, c) for z in range(nz)] for b in range(NY) for c in range(CORES)]
    core_groups = [[place(b, z, c) for b in range(NY) for z in range(nz)] for c in range(CORES)]
    chip_groups = [[place(b, z, c) for c in range(CORES)] for b in range(NY) for z in range(nz)]

    def along_y(x, step):
        return lax.ppermute(x, "space", [(place(y, z, c), place(y - step, z, c)) for y, z, c in where])

    def along_x(x, step):
        return lax.ppermute(x, "chan", [(a, (a - step) % chan) for a in range(chan)])

    def of_chip(x):
        return lax.all_gather(x, "space", axis=0, tiled=False, axis_index_groups=chip_groups)

    y = lax.axis_index("space") // (nz * CORES)
    core = lax.axis_index("space") % CORES
    turn = jnp.arange(NY, dtype=jnp.int32)
    x = lax.axis_index("chan")
    order = [(y + turn) % NY, core[None], (y + turn - x) % NY, (x + turn - y) % NY]
    order = jnp.concatenate(order).astype(jnp.int32)
    core = core[None]

    swapped = lax.ppermute(
        weights,
        ("space", "chan"),
        [(place(b, z, c) * chan + a, place(a, z, c) * chan + b) for b, z, c in where for a in range(chan)],
    )
    (shared,) = whole(
        prepare_kernel,
        [((SHARED, width), F32)],
        (block_count, features, cotangent, send_rows.T, rule_src, rule_dst),
        in_specs=[SMEM] + [HBM] * 5,
        scratch=[
            pltpu.VMEM((rows, width), F32),
            pltpu.VMEM((slots, peers), jnp.int32),
            pltpu.VMEM(rule_src.shape, jnp.int32),
            pltpu.VMEM(rule_dst.shape, jnp.int32),
            pltpu.SemaphoreType.DMA((5,)),
        ],
        mebibytes=SMALL,
    )
    shared = of_chip(shared).reshape(CORES * SHARED, width)
    swapped, shared = lax.optimization_barrier((swapped, shared))
    gathered = lax.all_gather(swapped, "space", axis=0, tiled=True, axis_index_groups=z_groups)
    (own,) = whole(regroup_kernel, [((offsets, 4 * nz, width), F32)], (gathered,), mebibytes=SMALL)
    shared, own = lax.optimization_barrier((shared, own))
    pieces = [own] + [along_y(own, s) for s in (1, 2, 3)]
    outgoing, cots, sends = whole(
        outgoing_kernel,
        [((halo_rows, width), F32), ((CORES * rows, width), F32), ((CORES * slots, peers), F32)],
        (core, shared),
        in_specs=[SMEM, VMEM],
        scratch=[pltpu.VMEM((peers, width), F32)],
        mebibytes=SMALL,
    )
    cots = [cots] + [along_x(cots, s) for s in (1, 2, 3)]

    def exchange(x):
        x = x.reshape(peers // CORES, CORES * slots, width)
        x = lax.all_to_all(
            x, "space", split_axis=0, concat_axis=0, tiled=True, axis_index_groups=core_groups
        )
        return x.reshape(halo_rows, width)

    incoming = exchange(outgoing)
    halo_grad, local_grad, other_parts, *parts = whole(
        core_kernel,
        [((halo_rows, width), F32), ((rows, width), F32), ((NY * rows, width), F32)]
        + [((rows, width), F32)] * NY,
        (order, shared, incoming, *cots, *pieces),
        in_specs=[SMEM] + [HBM] * (2 * NY + 2),
        out_specs=[HBM] + [VMEM] * 2 + [HBM] * NY,
        scratch=[
            pltpu.VMEM(shared.shape, F32),
            pltpu.VMEM(incoming.shape, F32),
            pltpu.VMEM((NY, CORES * rows, width), F32),
            pltpu.VMEM((NY, *own.shape), F32),
            pltpu.VMEM((NY * width, 2 * CORES * rows), BF16),
            pltpu.VMEM((table_rows, 2 * width), BF16),
            pltpu.VMEM((CORES, NY, rows, width), F32),
            pltpu.VMEM((halo_rows, width), F32),
            pltpu.SemaphoreType.DMA((2,)),
            pltpu.SemaphoreType.DMA((NY,)),
            pltpu.SemaphoreType.DMA((CHUNKS, NY)),
            pltpu.SemaphoreType.DMA((NY + 1,)),
        ],
        mebibytes=LARGE,
    )
    returned = exchange(halo_grad)
    other_parts = lax.dynamic_index_in_dim(of_chip(other_parts), 1 - core[0], 0, False)
    parts = [p + other_parts[s * rows : (s + 1) * rows] for s, p in enumerate(parts)]
    conv_out = parts[0] + along_x(parts[3], 1) + along_x(parts[2], 2) + along_x(parts[1], 3)
    own_grad, other_grad = whole(
        finish_kernel,
        [((rows, width), F32)] * 2,
        (core, local_grad, returned, sends),
        in_specs=[SMEM] + [VMEM] * 3,
        scratch=[pltpu.VMEM((peers, width), F32), pltpu.VMEM((CORES, rows, width), F32)],
        mebibytes=SMALL,
    )
    other_grad = lax.dynamic_index_in_dim(of_chip(other_grad), 1 - core[0], 0, False)
    return (conv_out, own_grad + other_grad)


def solution(mesh):
    placed = (
        P("space", "chan"),
        P(None, "space", "chan"),
        P("space", "chan"),
        P("space", None),
        P("space", None),
        P("space"),
        P("space", None),
    )
    return jax.shard_map(
        on_device,
        mesh=mesh,
        in_specs=placed,
        out_specs=(P("space", "chan"), P("space", "chan")),
        check_vma=False,
    )
```

```python
import jax
import jax.numpy as jnp
from jax import lax
from jax.experimental import pallas as pl
from jax.experimental.pallas import tpu as pltpu
from jax.sharding import PartitionSpec as P

F32 = jnp.float32
BF16 = jnp.bfloat16
NY = 4
CORES = 2
SPANS = ((0, 9), (9, 18), (18, 27))
CHUNKS = len(SPANS)
SMALL, LARGE = 16, 63


def iota(shape, dim):
    return lax.broadcasted_iota(jnp.int32, shape, dim)


def split2(x):
    high = x.astype(BF16)
    return high, (x - high.astype(F32)).astype(BF16)


def split3(x):
    high = x.astype(BF16)
    rest = x - high.astype(F32)
    middle = rest.astype(BF16)
    return high, middle, (rest - middle.astype(F32)).astype(BF16)


def dot(a, b):
    return jnp.dot(a, b, preferred_element_type=F32)


def chip_x():
    return lax.axis_index("chan")


def chip_y():
    return lax.axis_index("space") // (lax.axis_size("space") // NY)


def core_index():
    return lax.axis_index("space") % CORES


def as_onehot(mask):
    return jnp.where(mask, 1.0, 0.0).astype(BF16)


def pick_left(onehot, x):
    a, b, c = split3(x)
    return (dot(onehot, a) + dot(onehot, b)) + dot(onehot, c)


def pick_right(x, onehot):
    a, b, c = split3(x)
    return (dot(a, onehot) + dot(b, onehot)) + dot(c, onehot)


def to_inner(n):
    row = iota((n, n), 0)
    place = ((row >> 2) & 1) * 64 + (row >> 3) * 4 + (row & 3)
    return as_onehot(iota((n, n), 1) == place)


def from_inner(n):
    row = iota((n, n), 0)
    place = ((row >> 2) & 15) * 8 + (row >> 6) * 4 + (row & 3)
    return as_onehot(iota((n, n), 1) == place)


FEATURES, SOURCES, TARGETS, SENDS, SHARED = 128, 256, 288, 320, 328


def onehot_rows(line, rows):
    return as_onehot(line.astype(jnp.int32) == iota((rows, line.shape[1]), 0))


def started(pairs, sems):
    copies = [pltpu.make_async_copy(a, b, sems.at[i]) for i, (a, b) in enumerate(pairs)]
    for copy in copies:
        copy.start()
    return copies


def prepare_kernel(
    count_ref, features_in, cot_in, send_in, src_in, dst_in, shared_ref,
    features_ref, send_ref, src_ref, dst_ref, sems,
):
    rows, width = features_ref.shape
    offsets, block = src_ref.shape
    copies = started(
        [
            (features_in, features_ref),
            (send_in, send_ref),
            (src_in, src_ref),
            (dst_in, dst_ref),
            (cot_in, shared_ref.at[pl.ds(0, rows)]),
        ],
        sems,
    )
    for copy in copies:
        copy.wait()
    shared_ref[FEATURES : FEATURES + rows, :] = pick_right(features_ref[...], to_inner(width))
    shared_ref[SOURCES:SHARED, :] = jnp.zeros((SHARED - SOURCES, width), F32)
    for k in range(offsets):
        live = iota((1, block), 1) < count_ref[k]
        shared_ref[SOURCES + k : SOURCES + k + 1, :] = jnp.where(live, src_ref[k : k + 1, :], -1).astype(F32)
    shared_ref[TARGETS : TARGETS + offsets, :] = dst_ref[...].astype(F32)
    shared_ref[SENDS : SENDS + send_ref.shape[0], :] = send_ref[...].astype(F32)


def outgoing_kernel(shared_ref, outgoing_ref, cot_ref, sends_ref, picked_ref):
    rows, width = picked_ref.shape
    half = width // CORES
    slots = sends_ref.shape[0] // CORES
    chips = picked_ref.shape[0] // CORES
    for device in range(CORES):
        base = device * SHARED
        cot_ref[device * rows : (device + 1) * rows, :] = shared_ref[base : base + rows, :]
        inner = shared_ref[base + FEATURES : base + FEATURES + rows, :]
        parts = split3(pltpu.roll(inner, half * core_index(), axis=1))
        for slot in range(slots):
            line = shared_ref[base + SENDS + slot : base + SENDS + slot + 1, :]
            sends_ref[device * slots + slot : device * slots + slot + 1, :] = line
            onehot = onehot_rows(line, rows)
            a, b, c = (
                lax.dot_general(onehot, part, (((0,), (0,)), ((), ())), preferred_element_type=F32)
                for part in parts
            )
            picked_ref[...] = (a + b) + c
            both = [picked_ref[pl.ds(d, chips, stride=CORES), :][:, :half] for d in range(CORES)]
            outgoing_ref[pl.ds(device * slots + slot, chips, stride=CORES * slots), :] = jnp.concatenate(
                both, axis=1
            )


def regroup_kernel(gathered_ref, grouped_ref):
    offsets, inner, _ = grouped_ref.shape
    depth = gathered_ref.shape[1]
    for k in range(offsets):
        for z in range(inner // depth):
            grouped_ref[k, z * depth : (z + 1) * depth, :] = gathered_ref[z * offsets + k]


def pairs_of(shared_ref, device, k, local, rows):
    start = device * SHARED + k
    src = shared_ref[start + SOURCES : start + SOURCES + 1, :]
    dst = shared_ref[start + TARGETS : start + TARGETS + 1, :]
    mine = dst == iota((local, dst.shape[1]), 0).astype(F32)
    source = jnp.sum(jnp.where(mine, src + 1.0, 0.0), axis=1, keepdims=True)
    return as_onehot(iota((local, rows), 1) == source.astype(jnp.int32) - 1)


def kernel_rows(pieces):
    wide = jnp.concatenate(pieces, axis=2)
    return wide.reshape(wide.shape[0] * wide.shape[1], wide.shape[2])


def core_kernel(*refs):
    shared_in, incoming_in = refs[:2]
    cot_in = refs[2]
    piece_in = refs[3 : NY + 3]
    refs = refs[NY + 3 :]
    halo_out, local_ref, *part_outs = refs[: NY + 2]
    shared_ref, incoming_ref, cot_ref, pieces_ref, turned_ref, table_ref, total_ref, halo_ref = refs[
        NY + 2 : -4
    ]
    first_sems, cot_sems, piece_sems, out_sems = refs[-4:]
    both_rows, width = part_outs[0].shape
    rows = both_rows // CORES
    table_rows = table_ref.shape[0] // CORES
    half = pieces_ref.shape[2]
    x, y, core = chip_x(), chip_y(), core_index()

    def piece_copy(chunk, n):
        span = pl.ds(SPANS[chunk][0], SPANS[chunk][1] - SPANS[chunk][0])
        return pltpu.make_async_copy(piece_in[n].at[span], pieces_ref.at[n, span], piece_sems.at[chunk, n])

    shared_copy = pltpu.make_async_copy(shared_in, shared_ref, first_sems.at[0])
    incoming_copy = pltpu.make_async_copy(incoming_in, incoming_ref, first_sems.at[1])
    cots = [
        pltpu.make_async_copy(cot_in.at[(y + n) % NY], cot_ref.at[n], cot_sems.at[n]) for n in range(NY)
    ]
    for copy in [shared_copy, incoming_copy] + cots:
        copy.start()
    for chunk in range(CHUNKS):
        for n in range(NY):
            piece_copy(chunk, n).start()

    def pairs_at(chunk):
        return [
            jnp.concatenate(
                [pairs_of(shared_ref, d, k, rows, table_rows) for k in range(*SPANS[chunk])], axis=0
            )
            for d in range(CORES)
        ]

    shared_copy.wait()
    local = [
        pltpu.roll(
            shared_ref[d * SHARED + FEATURES : d * SHARED + FEATURES + rows, :], half * core, axis=1
        )[:, :half]
        for d in range(CORES)
    ]
    incoming_copy.wait()
    table = jnp.concatenate([jnp.concatenate(local, axis=1), incoming_ref[...]], axis=0)
    high, low = split2(table)
    table_ref[...] = jnp.zeros_like(table_ref)
    for d in range(CORES):
        mine = slice(d * half, (d + 1) * half)
        table_ref[d * table_rows : (d + 1) * table_rows, d * width : (d + 1) * width] = jnp.concatenate(
            [high[:, mine], low[:, mine]], axis=1
        )
    for copy in cots:
        copy.wait()
    for n in range(NY):
        high, low = split2(cot_ref[n].T)
        turned_ref[n * width : (n + 1) * width, :both_rows] = high
        turned_ref[n * width : (n + 1) * width, both_rows:] = low

    grads = [None] * CORES
    total = None
    for chunk in range(CHUNKS):
        step = SPANS[chunk][1] - SPANS[chunk][0]
        pairs = pairs_at(chunk)
        both = dot(jnp.concatenate(pairs, axis=1), table_ref[...]).astype(BF16)
        wide = [
            jnp.concatenate(
                [both[k * rows : (k + 1) * rows, d * width : (d + 1) * width] for k in range(step)], axis=1
            )
            for d in range(CORES)
        ]
        wide = jnp.concatenate(wide, axis=0)
        for n in range(NY):
            piece_copy(chunk, n).wait()
        span = slice(*SPANS[chunk])
        high, low = split2(kernel_rows([pieces_ref[n, span] for n in range(NY)]))

        def doubled(x):
            x = x.reshape(step, half, x.shape[1])
            return jnp.concatenate([x, x], axis=1).reshape(step * width, x.shape[2])

        product = dot(wide, doubled(high)) + dot(wide, doubled(low))
        total = product if chunk == 0 else total + product
        turned = dot(high, turned_ref[...])
        product = turned[:, :both_rows] + turned[:, both_rows:] + dot(low, turned_ref[:, :both_rows])
        product = product.reshape(step, half, both_rows)
        for device in range(CORES):
            side = jnp.concatenate(
                [product[k][:, device * rows : (device + 1) * rows] for k in range(step)], axis=1
            )
            both = dot(jnp.concatenate(split2(side), axis=0), pairs[device])
            both = both[:half] + both[half:]
            grads[device] = both if chunk == 0 else grads[device] + both
    table = jnp.concatenate(grads, axis=0).T
    halo_ref[...] = table[rows:, :]
    outs = [pltpu.make_async_copy(halo_ref, halo_out, out_sems.at[NY])]
    outs[0].start()
    local_ref[...] = table[:rows, :]
    for n in range(NY):
        total_ref[n] = total[:, n * width : (n + 1) * width]
    for s in range(NY):
        outs.append(
            pltpu.make_async_copy(total_ref.at[(x + s - y + NY) % NY], part_outs[s], out_sems.at[s])
        )
        outs[-1].start()
    for copy in outs:
        copy.wait()


def finish_kernel(local_ref, returned_ref, sends_ref, *refs):
    part_refs = refs[:NY]
    own_conv_ref, own_grad_ref, other_ref, grads_ref, convs_ref, full_ref = refs[NY:]
    rows, width = own_grad_ref.shape
    half = width // CORES
    slots = sends_ref.shape[0] // CORES
    chips = sends_ref.shape[1] // CORES
    core = core_index()
    conv = (part_refs[0][...] + part_refs[1][...]) + (part_refs[2][...] + part_refs[3][...])
    spread = from_inner(width)
    spread = jnp.where(core == 0, spread[:half, :], spread[half:, :])
    for device in range(CORES):
        convs_ref[device] = conv[device * rows : (device + 1) * rows, :]
        total = local_ref[:, device * half : (device + 1) * half]
        for slot in range(slots):
            line = device * slots + slot
            part = returned_ref[pl.ds(line, chips, stride=CORES * slots), :]
            for d in range(CORES):
                grads_ref[pl.ds(d, chips, stride=CORES), :half] = part[:, d * half : (d + 1) * half]
            onehot = onehot_rows(sends_ref[line : line + 1, :], rows)
            total = total + pick_left(onehot, grads_ref[:, :half])
        full_ref[device] = pick_right(total, spread)
    own_conv_ref[...] = convs_ref[core]
    own_grad_ref[...] = full_ref[core]
    other_ref[:rows, :] = convs_ref[1 - core]
    other_ref[rows:, :] = full_ref[1 - core]


VMEM = pl.BlockSpec(memory_space=pltpu.VMEM)
HBM = pl.BlockSpec(memory_space=pl.ANY)
SMEM = pl.BlockSpec(memory_space=pltpu.SMEM)


def params(mebibytes):
    return pltpu.CompilerParams(vmem_limit_bytes=mebibytes * 1024 * 1024)


def whole(kernel, outs, args, in_specs=None, out_specs=None, scratch=(), mebibytes=16):
    return pl.pallas_call(
        kernel,
        out_shape=tuple(jax.ShapeDtypeStruct(s, t) for s, t in outs),
        in_specs=in_specs or [VMEM] * len(args),
        out_specs=tuple(out_specs or [VMEM] * len(outs)),
        scratch_shapes=list(scratch),
        compiler_params=params(mebibytes),
    )(*args)


def on_device(features, weights, cotangent, rule_src, rule_dst, block_count, send_rows):
    space = lax.axis_size("space")
    chan = lax.axis_size("chan")
    nz = space // (NY * CORES)
    rows, width = features.shape
    offsets = weights.shape[0]
    peers, slots = send_rows.shape
    halo_rows = peers * slots
    table_rows = rows + halo_rows
    half = width // CORES

    def place(y, z, core):
        return ((y % NY) * nz + z) * CORES + core

    where = [(y, z, core) for y in range(NY) for z in range(nz) for core in range(CORES)]
    z_groups = [[place(b, z, c) for z in range(nz)] for b in range(NY) for c in range(CORES)]
    core_groups = [[place(b, z, c) for b in range(NY) for z in range(nz)] for c in range(CORES)]
    chip_groups = [[place(b, z, c) for c in range(CORES)] for b in range(NY) for z in range(nz)]

    def along_y(x, step):
        return lax.ppermute(x, "space", [(place(y, z, c), place(y - step, z, c)) for y, z, c in where])

    def along_x(x, step):
        return lax.ppermute(x, "chan", [(a, (a - step) % chan) for a in range(chan)])

    def of_chip(x):
        return lax.all_gather(x, "space", axis=0, tiled=False, axis_index_groups=chip_groups)

    swapped = lax.ppermute(
        weights,
        ("space", "chan"),
        [(place(b, z, c) * chan + a, place(a, z, c) * chan + b) for b, z, c in where for a in range(chan)],
    )
    (shared,) = whole(
        prepare_kernel,
        [((SHARED, width), F32)],
        (block_count, features, cotangent, send_rows.T, rule_src, rule_dst),
        in_specs=[SMEM] + [HBM] * 5,
        scratch=[
            pltpu.VMEM((rows, width), F32),
            pltpu.VMEM((slots, peers), jnp.int32),
            pltpu.VMEM(rule_src.shape, jnp.int32),
            pltpu.VMEM(rule_dst.shape, jnp.int32),
            pltpu.SemaphoreType.DMA((5,)),
        ],
        mebibytes=SMALL,
    )
    shared = of_chip(shared).reshape(CORES * SHARED, width)
    swapped, shared = lax.optimization_barrier((swapped, shared))
    gathered = lax.all_gather(swapped, "space", axis=0, tiled=True, axis_index_groups=z_groups)
    (own,) = whole(regroup_kernel, [((offsets, 4 * nz, width), F32)], (gathered,), mebibytes=SMALL)
    shared, own = lax.optimization_barrier((shared, own))
    pieces = [own] + [along_y(own, s) for s in (1, 2, 3)]
    outgoing, cots, sends = whole(
        outgoing_kernel,
        [((halo_rows, width), F32), ((CORES * rows, width), F32), ((CORES * slots, peers), F32)],
        (shared,),
        scratch=[pltpu.VMEM((peers, width), F32)],
        mebibytes=SMALL,
    )
    cots = lax.all_gather(cots, "chan", axis=0, tiled=False)

    def exchange(x):
        x = x.reshape(peers // CORES, CORES * slots, width)
        x = lax.all_to_all(
            x, "space", split_axis=0, concat_axis=0, tiled=True, axis_index_groups=core_groups
        )
        return x.reshape(halo_rows, width)

    incoming = exchange(outgoing)
    halo_grad, local_grad, *parts = whole(
        core_kernel,
        [((halo_rows, width), F32), ((rows, width), F32)] + [((CORES * rows, width), F32)] * NY,
        (shared, incoming, cots, *pieces),
        in_specs=[HBM] * (NY + 3),
        out_specs=[HBM, VMEM] + [HBM] * NY,
        scratch=[
            pltpu.VMEM(shared.shape, F32),
            pltpu.VMEM(incoming.shape, F32),
            pltpu.VMEM((NY, CORES * rows, width), F32),
            pltpu.VMEM((NY, *own.shape), F32),
            pltpu.VMEM((NY * width, 2 * CORES * rows), BF16),
            pltpu.VMEM((CORES * table_rows, 2 * width), BF16),
            pltpu.VMEM((NY, CORES * rows, width), F32),
            pltpu.VMEM((halo_rows, width), F32),
            pltpu.SemaphoreType.DMA((2,)),
            pltpu.SemaphoreType.DMA((NY,)),
            pltpu.SemaphoreType.DMA((CHUNKS, NY)),
            pltpu.SemaphoreType.DMA((NY + 1,)),
        ],
        mebibytes=LARGE,
    )
    returned = exchange(halo_grad)
    parts = [parts[0]] + [along_x(parts[NY - s], s) for s in (1, 2, 3)]
    own_conv, own_grad, other = whole(
        finish_kernel,
        [((rows, width), F32)] * 2 + [((CORES * rows, width), F32)],
        (local_grad, returned, sends, *parts),
        scratch=[
            pltpu.VMEM((peers, width), F32),
            pltpu.VMEM((CORES, rows, width), F32),
            pltpu.VMEM((CORES, rows, width), F32),
        ],
        mebibytes=SMALL,
    )
    core = lax.axis_index("space") % CORES
    other = lax.dynamic_index_in_dim(of_chip(other), 1 - core, 0, False)
    return (own_conv + other[:rows], own_grad + other[rows:])


def solution(mesh):
    placed = (
        P("space", "chan"),
        P(None, "space", "chan"),
        P("space", "chan"),
        P("space", None),
        P("space", None),
        P("space"),
        P("space", None),
    )
    return jax.shard_map(
        on_device,
        mesh=mesh,
        in_specs=placed,
        out_specs=(P("space", "chan"), P("space", "chan")),
        check_vma=False,
    )
```

```python
import jax
import jax.numpy as jnp
from jax import lax
from jax.experimental import pallas as pl
from jax.experimental.pallas import tpu as pltpu
from jax.sharding import PartitionSpec as P

F32 = jnp.float32
BF16 = jnp.bfloat16
NY = 4
CORES = 2
SPANS = ((0, 6), (6, 27))
CHUNKS = len(SPANS)
SMALL, LARGE = 16, 63


def iota(shape, dim):
    return lax.broadcasted_iota(jnp.int32, shape, dim)


def split2(x):
    high = x.astype(BF16)
    return high, (x - high.astype(F32)).astype(BF16)


def split3(x):
    high = x.astype(BF16)
    rest = x - high.astype(F32)
    middle = rest.astype(BF16)
    return high, middle, (rest - middle.astype(F32)).astype(BF16)


def dot(a, b):
    return jnp.dot(a, b, preferred_element_type=F32)


def chip_x():
    return lax.axis_index("chan")


def chip_y():
    return lax.axis_index("space") // (lax.axis_size("space") // NY)


def core_index():
    return lax.axis_index("space") % CORES


def as_onehot(mask):
    return jnp.where(mask, 1.0, 0.0).astype(BF16)


def pick_left(onehot, x):
    a, b, c = split3(x)
    return (dot(onehot, a) + dot(onehot, b)) + dot(onehot, c)


def pick_right(x, onehot):
    a, b, c = split3(x)
    return (dot(a, onehot) + dot(b, onehot)) + dot(c, onehot)


def to_inner(n):
    row = iota((n, n), 0)
    place = ((row >> 2) & 1) * 64 + (row >> 3) * 4 + (row & 3)
    return as_onehot(iota((n, n), 1) == place)


def from_inner(n):
    row = iota((n, n), 0)
    place = ((row >> 2) & 15) * 8 + (row >> 6) * 4 + (row & 3)
    return as_onehot(iota((n, n), 1) == place)


FEATURES, SOURCES, TARGETS, SENDS, SHARED = 128, 256, 288, 320, 328


def onehot_rows(line, rows):
    return as_onehot(line.astype(jnp.int32) == iota((rows, line.shape[1]), 0))


def started(pairs, sems):
    copies = [pltpu.make_async_copy(a, b, sems.at[i]) for i, (a, b) in enumerate(pairs)]
    for copy in copies:
        copy.start()
    return copies


def prepare_kernel(
    count_ref, features_in, cot_in, send_in, src_in, dst_in, shared_ref,
    features_ref, send_ref, src_ref, dst_ref, sems,
):
    rows, width = features_ref.shape
    offsets, block = src_ref.shape
    copies = started(
        [
            (features_in, features_ref),
            (send_in, send_ref),
            (src_in, src_ref),
            (dst_in, dst_ref),
            (cot_in, shared_ref.at[pl.ds(0, rows)]),
        ],
        sems,
    )
    for copy in copies:
        copy.wait()
    shared_ref[FEATURES : FEATURES + rows, :] = pick_right(features_ref[...], to_inner(width))
    shared_ref[SOURCES:SHARED, :] = jnp.zeros((SHARED - SOURCES, width), F32)
    for k in range(offsets):
        live = iota((1, block), 1) < count_ref[k]
        shared_ref[SOURCES + k : SOURCES + k + 1, :] = jnp.where(live, src_ref[k : k + 1, :], -1).astype(F32)
    shared_ref[TARGETS : TARGETS + offsets, :] = dst_ref[...].astype(F32)
    shared_ref[SENDS : SENDS + send_ref.shape[0], :] = send_ref[...].astype(F32)


def outgoing_kernel(shared_ref, outgoing_ref, cot_ref, sends_ref, picked_ref):
    rows, width = picked_ref.shape
    half = width // CORES
    slots = sends_ref.shape[0] // CORES
    chips = picked_ref.shape[0] // CORES
    for device in range(CORES):
        base = device * SHARED
        cot_ref[device * rows : (device + 1) * rows, :] = shared_ref[base : base + rows, :]
        inner = shared_ref[base + FEATURES : base + FEATURES + rows, :]
        parts = split3(pltpu.roll(inner, half * core_index(), axis=1))
        for slot in range(slots):
            line = shared_ref[base + SENDS + slot : base + SENDS + slot + 1, :]
            sends_ref[device * slots + slot : device * slots + slot + 1, :] = line
            onehot = onehot_rows(line, rows)
            a, b, c = (
                lax.dot_general(onehot, part, (((0,), (0,)), ((), ())), preferred_element_type=F32)
                for part in parts
            )
            picked_ref[...] = (a + b) + c
            both = [picked_ref[pl.ds(d, chips, stride=CORES), :][:, :half] for d in range(CORES)]
            outgoing_ref[pl.ds(device * slots + slot, chips, stride=CORES * slots), :] = jnp.concatenate(
                both, axis=1
            )


def regroup_kernel(gathered_ref, grouped_ref):
    offsets, inner, _ = grouped_ref.shape
    depth = gathered_ref.shape[1]
    for k in range(offsets):
        for z in range(inner // depth):
            grouped_ref[k, z * depth : (z + 1) * depth, :] = gathered_ref[z * offsets + k]


def pairs_of(shared_ref, device, k, local, rows):
    start = device * SHARED + k
    src = shared_ref[start + SOURCES : start + SOURCES + 1, :]
    dst = shared_ref[start + TARGETS : start + TARGETS + 1, :]
    mine = dst == iota((local, dst.shape[1]), 0).astype(F32)
    source = jnp.sum(jnp.where(mine, src + 1.0, 0.0), axis=1, keepdims=True)
    return as_onehot(iota((local, rows), 1) == source.astype(jnp.int32) - 1)


def kernel_rows(pieces):
    wide = jnp.concatenate(pieces, axis=2)
    return wide.reshape(wide.shape[0] * wide.shape[1], wide.shape[2])


def core_kernel(*refs):
    shared_in, incoming_in = refs[:2]
    cot_in = refs[2]
    piece_in = refs[3 : NY + 3]
    refs = refs[NY + 3 :]
    halo_out, local_ref, *part_outs = refs[: NY + 2]
    shared_ref, incoming_ref, cot_ref, pieces_ref, turned_ref, table_ref, total_ref, halo_ref = refs[
        NY + 2 : -4
    ]
    first_sems, cot_sems, piece_sems, out_sems = refs[-4:]
    both_rows, width = part_outs[0].shape
    rows = both_rows // CORES
    table_rows = table_ref.shape[0] // CORES
    half = pieces_ref.shape[2]
    x, y, core = chip_x(), chip_y(), core_index()

    def piece_copy(chunk, n):
        span = pl.ds(SPANS[chunk][0], SPANS[chunk][1] - SPANS[chunk][0])
        return pltpu.make_async_copy(piece_in[n].at[span], pieces_ref.at[n, span], piece_sems.at[chunk, n])

    shared_copy = pltpu.make_async_copy(shared_in, shared_ref, first_sems.at[0])
    incoming_copy = pltpu.make_async_copy(incoming_in, incoming_ref, first_sems.at[1])
    cots = [
        pltpu.make_async_copy(cot_in.at[(y + n) % NY], cot_ref.at[n], cot_sems.at[n]) for n in range(NY)
    ]
    for copy in [shared_copy, incoming_copy] + cots:
        copy.start()
    def pairs_at(chunk):
        return [
            jnp.concatenate(
                [pairs_of(shared_ref, d, k, rows, table_rows) for k in range(*SPANS[chunk])], axis=0
            )
            for d in range(CORES)
        ]

    shared_copy.wait()
    for chunk in range(CHUNKS):
        for n in range(NY):
            piece_copy(chunk, n).start()
    local = [
        pltpu.roll(
            shared_ref[d * SHARED + FEATURES : d * SHARED + FEATURES + rows, :], half * core, axis=1
        )[:, :half]
        for d in range(CORES)
    ]
    incoming_copy.wait()
    table = jnp.concatenate([jnp.concatenate(local, axis=1), incoming_ref[...]], axis=0)
    high, low = split2(table)
    table_ref[...] = jnp.zeros_like(table_ref)
    for d in range(CORES):
        mine = slice(d * half, (d + 1) * half)
        table_ref[d * table_rows : (d + 1) * table_rows, d * width : (d + 1) * width] = jnp.concatenate(
            [high[:, mine], low[:, mine]], axis=1
        )
    for copy in cots:
        copy.wait()
    for n in range(NY):
        high, low = split2(cot_ref[n].T)
        turned_ref[n * width : (n + 1) * width, :both_rows] = high
        turned_ref[n * width : (n + 1) * width, both_rows:] = low

    grads = [None] * CORES
    total = None
    for chunk in range(CHUNKS):
        step = SPANS[chunk][1] - SPANS[chunk][0]
        pairs = pairs_at(chunk)
        both = dot(jnp.concatenate(pairs, axis=1), table_ref[...]).astype(BF16)
        wide = [
            jnp.concatenate(
                [both[k * rows : (k + 1) * rows, d * width : (d + 1) * width] for k in range(step)], axis=1
            )
            for d in range(CORES)
        ]
        wide = jnp.concatenate(wide, axis=0)
        for n in range(NY):
            piece_copy(chunk, n).wait()
        span = slice(*SPANS[chunk])
        high, low = split2(kernel_rows([pieces_ref[n, span] for n in range(NY)]))

        def doubled(x):
            x = x.reshape(step, half, x.shape[1])
            return jnp.concatenate([x, x], axis=1).reshape(step * width, x.shape[2])

        highs = jnp.concatenate([wide[:, k * width : k * width + half] for k in range(step)], axis=1)
        product = dot(wide, doubled(high)) + dot(highs, low)
        total = product if chunk == 0 else total + product
        if chunk == CHUNKS - 1:
            outs = []
            for n in range(NY):
                total_ref[n] = total[:, n * width : (n + 1) * width]
            for s in range(NY):
                outs.append(
                    pltpu.make_async_copy(total_ref.at[(x + s - y + NY) % NY], part_outs[s], out_sems.at[s])
                )
                outs[-1].start()
        turned = dot(high, turned_ref[...])
        product = turned[:, :both_rows] + turned[:, both_rows:] + dot(low, turned_ref[:, :both_rows])
        product = product.reshape(step, half, both_rows)
        for device in range(CORES):
            side = jnp.concatenate(
                [product[k][:, device * rows : (device + 1) * rows] for k in range(step)], axis=1
            )
            both = dot(jnp.concatenate(split2(side), axis=0), pairs[device])
            both = both[:half] + both[half:]
            grads[device] = both if chunk == 0 else grads[device] + both
    table = jnp.concatenate(grads, axis=0).T
    halo_ref[...] = table[rows:, :]
    outs.append(pltpu.make_async_copy(halo_ref, halo_out, out_sems.at[NY]))
    outs[-1].start()
    local_ref[...] = table[:rows, :]
    for copy in outs:
        copy.wait()


def finish_kernel(local_ref, returned_ref, sends_ref, *refs):
    part_refs = refs[:NY]
    own_conv_ref, own_grad_ref, other_ref, grads_ref, convs_ref, full_ref = refs[NY:]
    rows, width = own_grad_ref.shape
    half = width // CORES
    slots = sends_ref.shape[0] // CORES
    chips = sends_ref.shape[1] // CORES
    core = core_index()
    conv = (part_refs[0][...] + part_refs[1][...]) + (part_refs[2][...] + part_refs[3][...])
    spread = from_inner(width)
    spread = jnp.where(core == 0, spread[:half, :], spread[half:, :])
    for device in range(CORES):
        convs_ref[device] = conv[device * rows : (device + 1) * rows, :]
        total = local_ref[:, device * half : (device + 1) * half]
        for slot in range(slots):
            line = device * slots + slot
            part = returned_ref[pl.ds(line, chips, stride=CORES * slots), :]
            for d in range(CORES):
                grads_ref[pl.ds(d, chips, stride=CORES), :half] = part[:, d * half : (d + 1) * half]
            onehot = onehot_rows(sends_ref[line : line + 1, :], rows)
            total = total + pick_left(onehot, grads_ref[:, :half])
        full_ref[device] = pick_right(total, spread)
    own_conv_ref[...] = convs_ref[core]
    own_grad_ref[...] = full_ref[core]
    other_ref[:rows, :] = convs_ref[1 - core]
    other_ref[rows:, :] = full_ref[1 - core]


VMEM = pl.BlockSpec(memory_space=pltpu.VMEM)
HBM = pl.BlockSpec(memory_space=pl.ANY)
SMEM = pl.BlockSpec(memory_space=pltpu.SMEM)


def params(mebibytes):
    return pltpu.CompilerParams(vmem_limit_bytes=mebibytes * 1024 * 1024)


def whole(kernel, outs, args, in_specs=None, out_specs=None, scratch=(), mebibytes=16):
    return pl.pallas_call(
        kernel,
        out_shape=tuple(jax.ShapeDtypeStruct(s, t) for s, t in outs),
        in_specs=in_specs or [VMEM] * len(args),
        out_specs=tuple(out_specs or [VMEM] * len(outs)),
        scratch_shapes=list(scratch),
        compiler_params=params(mebibytes),
    )(*args)


def on_device(features, weights, cotangent, rule_src, rule_dst, block_count, send_rows):
    space = lax.axis_size("space")
    chan = lax.axis_size("chan")
    nz = space // (NY * CORES)
    rows, width = features.shape
    offsets = weights.shape[0]
    peers, slots = send_rows.shape
    halo_rows = peers * slots
    table_rows = rows + halo_rows
    half = width // CORES

    def place(y, z, core):
        return ((y % NY) * nz + z) * CORES + core

    where = [(y, z, core) for y in range(NY) for z in range(nz) for core in range(CORES)]
    z_groups = [[place(b, z, c) for z in range(nz)] for b in range(NY) for c in range(CORES)]
    core_groups = [[place(b, z, c) for b in range(NY) for z in range(nz)] for c in range(CORES)]
    chip_groups = [[place(b, z, c) for c in range(CORES)] for b in range(NY) for z in range(nz)]

    def along_y(x, step):
        return lax.ppermute(x, "space", [(place(y, z, c), place(y - step, z, c)) for y, z, c in where])

    def along_x(x, step):
        return lax.ppermute(x, "chan", [(a, (a - step) % chan) for a in range(chan)])

    def of_chip(x):
        return lax.all_gather(x, "space", axis=0, tiled=False, axis_index_groups=chip_groups)

    swapped = lax.ppermute(
        weights,
        ("space", "chan"),
        [(place(b, z, c) * chan + a, place(a, z, c) * chan + b) for b, z, c in where for a in range(chan)],
    )
    (shared,) = whole(
        prepare_kernel,
        [((SHARED, width), F32)],
        (block_count, features, cotangent, send_rows.T, rule_src, rule_dst),
        in_specs=[SMEM] + [HBM] * 5,
        scratch=[
            pltpu.VMEM((rows, width), F32),
            pltpu.VMEM((slots, peers), jnp.int32),
            pltpu.VMEM(rule_src.shape, jnp.int32),
            pltpu.VMEM(rule_dst.shape, jnp.int32),
            pltpu.SemaphoreType.DMA((5,)),
        ],
        mebibytes=SMALL,
    )
    shared = of_chip(shared).reshape(CORES * SHARED, width)
    swapped, shared = lax.optimization_barrier((swapped, shared))
    gathered = lax.all_gather(swapped, "space", axis=0, tiled=True, axis_index_groups=z_groups)
    (own,) = whole(regroup_kernel, [((offsets, 4 * nz, width), F32)], (gathered,), mebibytes=SMALL)
    shared, own = lax.optimization_barrier((shared, own))
    pieces = [own] + [along_y(own, s) for s in (1, 2, 3)]
    outgoing, cots, sends = whole(
        outgoing_kernel,
        [((halo_rows, width), F32), ((CORES * rows, width), F32), ((CORES * slots, peers), F32)],
        (shared,),
        scratch=[pltpu.VMEM((peers, width), F32)],
        mebibytes=SMALL,
    )
    cots = lax.all_gather(cots, "chan", axis=0, tiled=False)

    def exchange(x):
        x = x.reshape(peers // CORES, CORES * slots, width)
        x = lax.all_to_all(
            x, "space", split_axis=0, concat_axis=0, tiled=True, axis_index_groups=core_groups
        )
        return x.reshape(halo_rows, width)

    incoming = exchange(outgoing)
    halo_grad, local_grad, *parts = whole(
        core_kernel,
        [((halo_rows, width), F32), ((rows, width), F32)] + [((CORES * rows, width), F32)] * NY,
        (shared, incoming, cots, *pieces),
        in_specs=[HBM] * (NY + 3),
        out_specs=[HBM, VMEM] + [HBM] * NY,
        scratch=[
            pltpu.VMEM(shared.shape, F32),
            pltpu.VMEM(incoming.shape, F32),
            pltpu.VMEM((NY, CORES * rows, width), F32),
            pltpu.VMEM((NY, *own.shape), F32),
            pltpu.VMEM((NY * width, 2 * CORES * rows), BF16),
            pltpu.VMEM((CORES * table_rows, 2 * width), BF16),
            pltpu.VMEM((NY, CORES * rows, width), F32),
            pltpu.VMEM((halo_rows, width), F32),
            pltpu.SemaphoreType.DMA((2,)),
            pltpu.SemaphoreType.DMA((NY,)),
            pltpu.SemaphoreType.DMA((CHUNKS, NY)),
            pltpu.SemaphoreType.DMA((NY + 1,)),
        ],
        mebibytes=LARGE,
    )
    returned = exchange(halo_grad)
    parts = [parts[0]] + [along_x(parts[NY - s], s) for s in (2, 1, 3)]
    own_conv, own_grad, other = whole(
        finish_kernel,
        [((rows, width), F32)] * 2 + [((CORES * rows, width), F32)],
        (local_grad, returned, sends, *parts),
        scratch=[
            pltpu.VMEM((peers, width), F32),
            pltpu.VMEM((CORES, rows, width), F32),
            pltpu.VMEM((CORES, rows, width), F32),
        ],
        mebibytes=SMALL,
    )
    core = lax.axis_index("space") % CORES
    other = lax.dynamic_index_in_dim(of_chip(other), 1 - core, 0, False)
    return (own_conv + other[:rows], own_grad + other[rows:])


def solution(mesh):
    placed = (
        P("space", "chan"),
        P(None, "space", "chan"),
        P("space", "chan"),
        P("space", None),
        P("space", None),
        P("space"),
        P("space", None),
    )
    return jax.shard_map(
        on_device,
        mesh=mesh,
        in_specs=placed,
        out_specs=(P("space", "chan"), P("space", "chan")),
        check_vma=False,
    )
```

```python
import jax
import jax.numpy as jnp
from jax import lax
from jax.experimental import pallas as pl
from jax.experimental.pallas import tpu as pltpu
from jax.sharding import PartitionSpec as P

F32 = jnp.float32
BF16 = jnp.bfloat16
NY = 4
CORES = 2
SPANS = ((0, 6), (6, 27))
CHUNKS = len(SPANS)
SMALL, LARGE = 16, 63


def iota(shape, dim):
    return lax.broadcasted_iota(jnp.int32, shape, dim)


def split2(x):
    high = x.astype(BF16)
    return high, (x - high.astype(F32)).astype(BF16)


def split3(x):
    high = x.astype(BF16)
    rest = x - high.astype(F32)
    middle = rest.astype(BF16)
    return high, middle, (rest - middle.astype(F32)).astype(BF16)


def dot(a, b):
    return jnp.dot(a, b, preferred_element_type=F32)


def chip_x():
    return lax.axis_index("chan")


def chip_y():
    return lax.axis_index("space") // (lax.axis_size("space") // NY)


def core_index():
    return lax.axis_index("space") % CORES


def as_onehot(mask):
    return jnp.where(mask, 1.0, 0.0).astype(BF16)


def pick_left(onehot, x):
    a, b, c = split3(x)
    return (dot(onehot, a) + dot(onehot, b)) + dot(onehot, c)


def pick_right(x, onehot):
    a, b, c = split3(x)
    return (dot(a, onehot) + dot(b, onehot)) + dot(c, onehot)


def to_inner(n):
    row = iota((n, n), 0)
    place = ((row >> 2) & 1) * 64 + (row >> 3) * 4 + (row & 3)
    return as_onehot(iota((n, n), 1) == place)


def from_inner(n):
    row = iota((n, n), 0)
    place = ((row >> 2) & 15) * 8 + (row >> 6) * 4 + (row & 3)
    return as_onehot(iota((n, n), 1) == place)


FEATURES, SOURCES, TARGETS, SENDS, SHARED = 128, 256, 288, 320, 328


def onehot_rows(line, rows):
    return as_onehot(line.astype(jnp.int32) == iota((rows, line.shape[1]), 0))


def started(pairs, sems):
    copies = [pltpu.make_async_copy(a, b, sems.at[i]) for i, (a, b) in enumerate(pairs)]
    for copy in copies:
        copy.start()
    return copies


def prepare_kernel(
    count_ref, features_in, cot_in, send_in, src_in, dst_in, shared_ref,
    features_ref, send_ref, src_ref, dst_ref, sems,
):
    rows, width = features_ref.shape
    offsets, block = src_ref.shape
    copies = started(
        [
            (features_in, features_ref),
            (send_in, send_ref),
            (src_in, src_ref),
            (dst_in, dst_ref),
            (cot_in, shared_ref.at[pl.ds(0, rows)]),
        ],
        sems,
    )
    for copy in copies:
        copy.wait()
    shared_ref[FEATURES : FEATURES + rows, :] = pick_right(features_ref[...], to_inner(width))
    shared_ref[SOURCES:SHARED, :] = jnp.zeros((SHARED - SOURCES, width), F32)
    for k in range(offsets):
        live = iota((1, block), 1) < count_ref[k]
        shared_ref[SOURCES + k : SOURCES + k + 1, :] = jnp.where(live, src_ref[k : k + 1, :], -1).astype(F32)
    shared_ref[TARGETS : TARGETS + offsets, :] = dst_ref[...].astype(F32)
    shared_ref[SENDS : SENDS + send_ref.shape[0], :] = send_ref[...].astype(F32)


def outgoing_kernel(shared_ref, outgoing_ref, cot_ref, sends_ref, picked_ref):
    rows, width = picked_ref.shape
    half = width // CORES
    slots = sends_ref.shape[0] // CORES
    chips = picked_ref.shape[0] // CORES
    for device in range(CORES):
        base = device * SHARED
        cot_ref[device * rows : (device + 1) * rows, :] = shared_ref[base : base + rows, :]
        inner = shared_ref[base + FEATURES : base + FEATURES + rows, :]
        parts = split3(pltpu.roll(inner, half * core_index(), axis=1))
        for slot in range(slots):
            line = shared_ref[base + SENDS + slot : base + SENDS + slot + 1, :]
            sends_ref[device * slots + slot : device * slots + slot + 1, :] = line
            onehot = onehot_rows(line, rows)
            a, b, c = (
                lax.dot_general(onehot, part, (((0,), (0,)), ((), ())), preferred_element_type=F32)
                for part in parts
            )
            picked_ref[...] = (a + b) + c
            both = [picked_ref[pl.ds(d, chips, stride=CORES), :][:, :half] for d in range(CORES)]
            outgoing_ref[pl.ds(device * slots + slot, chips, stride=CORES * slots), :] = jnp.concatenate(
                both, axis=1
            )


def regroup_kernel(gathered_ref, grouped_ref):
    offsets, inner, _ = grouped_ref.shape
    depth = gathered_ref.shape[1]
    for k in range(offsets):
        for z in range(inner // depth):
            grouped_ref[k, z * depth : (z + 1) * depth, :] = gathered_ref[z * offsets + k]


def pairs_of(shared_ref, device, k, local, rows):
    start = device * SHARED + k
    src = shared_ref[start + SOURCES : start + SOURCES + 1, :]
    dst = shared_ref[start + TARGETS : start + TARGETS + 1, :]
    mine = dst == iota((local, dst.shape[1]), 0).astype(F32)
    source = jnp.sum(jnp.where(mine, src + 1.0, 0.0), axis=1, keepdims=True)
    return as_onehot(iota((local, rows), 1) == source.astype(jnp.int32) - 1)


def kernel_rows(pieces):
    wide = jnp.concatenate(pieces, axis=2)
    return wide.reshape(wide.shape[0] * wide.shape[1], wide.shape[2])


def core_kernel(*refs):
    shared_in, incoming_in = refs[:2]
    cot_in = refs[2]
    piece_in = refs[3 : NY + 3]
    refs = refs[NY + 3 :]
    halo_out, local_ref, *part_outs = refs[: NY + 2]
    shared_ref, incoming_ref, cot_ref, pieces_ref, turned_ref, table_ref, total_ref, halo_ref = refs[
        NY + 2 : -4
    ]
    first_sems, cot_sems, piece_sems, out_sems = refs[-4:]
    both_rows, width = part_outs[0].shape
    rows = both_rows // CORES
    table_rows = table_ref.shape[0] // CORES
    half = pieces_ref.shape[2]
    x, y, core = chip_x(), chip_y(), core_index()

    def piece_copy(chunk, n):
        span = pl.ds(SPANS[chunk][0], SPANS[chunk][1] - SPANS[chunk][0])
        return pltpu.make_async_copy(piece_in[n].at[span], pieces_ref.at[n, span], piece_sems.at[chunk, n])

    shared_copy = pltpu.make_async_copy(shared_in, shared_ref, first_sems.at[0])
    incoming_copy = pltpu.make_async_copy(incoming_in, incoming_ref, first_sems.at[1])
    cots = [
        pltpu.make_async_copy(cot_in.at[(y + n) % NY], cot_ref.at[n], cot_sems.at[n]) for n in range(NY)
    ]
    for copy in [shared_copy, incoming_copy] + cots:
        copy.start()
    def pairs_at(chunk):
        return [
            jnp.concatenate(
                [pairs_of(shared_ref, d, k, rows, table_rows) for k in range(*SPANS[chunk])], axis=0
            )
            for d in range(CORES)
        ]

    shared_copy.wait()
    for chunk in range(CHUNKS):
        for n in range(NY):
            piece_copy(chunk, n).start()
    local = [
        pltpu.roll(
            shared_ref[d * SHARED + FEATURES : d * SHARED + FEATURES + rows, :], half * core, axis=1
        )[:, :half]
        for d in range(CORES)
    ]
    incoming_copy.wait()
    table = jnp.concatenate([jnp.concatenate(local, axis=1), incoming_ref[...]], axis=0)
    high, low = split2(table)
    table_ref[...] = jnp.zeros_like(table_ref)
    for d in range(CORES):
        mine = slice(d * half, (d + 1) * half)
        table_ref[d * table_rows : (d + 1) * table_rows, d * width : (d + 1) * width] = jnp.concatenate(
            [high[:, mine], low[:, mine]], axis=1
        )
    for copy in cots:
        copy.wait()
    for n in range(NY):
        high, low = split2(cot_ref[n].T)
        turned_ref[n * width : (n + 1) * width, :both_rows] = high
        turned_ref[n * width : (n + 1) * width, both_rows:] = low

    grads = [None] * CORES
    total = None
    for chunk in range(CHUNKS):
        step = SPANS[chunk][1] - SPANS[chunk][0]
        pairs = pairs_at(chunk)
        both = dot(jnp.concatenate(pairs, axis=1), table_ref[...]).astype(BF16)
        wide = [
            jnp.concatenate(
                [both[k * rows : (k + 1) * rows, d * width : (d + 1) * width] for k in range(step)], axis=1
            )
            for d in range(CORES)
        ]
        wide = jnp.concatenate(wide, axis=0)
        for n in range(NY):
            piece_copy(chunk, n).wait()
        span = slice(*SPANS[chunk])
        high, low = split2(kernel_rows([pieces_ref[n, span] for n in range(NY)]))

        def doubled(x):
            x = x.reshape(step, half, x.shape[1])
            return jnp.concatenate([x, x], axis=1).reshape(step * width, x.shape[2])

        highs = jnp.concatenate([wide[:, k * width : k * width + half] for k in range(step)], axis=1)
        product = dot(wide, doubled(high)) + dot(highs, low)
        total = product if chunk == 0 else total + product
        if chunk == CHUNKS - 1:
            outs = []
            for n in range(NY):
                total_ref[n] = total[:, n * width : (n + 1) * width]
            for s in range(NY):
                outs.append(
                    pltpu.make_async_copy(total_ref.at[(x + s - y + NY) % NY], part_outs[s], out_sems.at[s])
                )
                outs[-1].start()
        turned = dot(high, turned_ref[...])
        product = turned[:, :both_rows] + turned[:, both_rows:] + dot(low, turned_ref[:, :both_rows])
        product = product.reshape(step, half, both_rows)
        for device in range(CORES):
            side = jnp.concatenate(
                [product[k][:, device * rows : (device + 1) * rows] for k in range(step)], axis=1
            )
            both = dot(jnp.concatenate(split2(side), axis=0), pairs[device])
            both = both[:half] + both[half:]
            grads[device] = both if chunk == 0 else grads[device] + both
    table = jnp.concatenate(grads, axis=0).T
    halo_ref[...] = table[rows:, :]
    outs.append(pltpu.make_async_copy(halo_ref, halo_out, out_sems.at[NY]))
    outs[-1].start()
    local_ref[...] = table[:rows, :]
    for copy in outs:
        copy.wait()


def finish_kernel(local_ref, returned_ref, sends_ref, *refs):
    part_refs = refs[:NY]
    own_conv_ref, own_grad_ref, other_ref, grads_ref, convs_ref, full_ref = refs[NY:]
    rows, width = own_grad_ref.shape
    half = width // CORES
    slots = sends_ref.shape[0] // CORES
    chips = sends_ref.shape[1] // CORES
    core = core_index()
    conv = (part_refs[0][...] + part_refs[1][...]) + (part_refs[2][...] + part_refs[3][...])
    spread = from_inner(width)
    spread = jnp.where(core == 0, spread[:half, :], spread[half:, :])
    for device in range(CORES):
        convs_ref[device] = conv[device * rows : (device + 1) * rows, :]
        total = local_ref[:, device * half : (device + 1) * half]
        for slot in range(slots):
            line = device * slots + slot
            part = returned_ref[pl.ds(line, chips, stride=CORES * slots), :]
            for d in range(CORES):
                grads_ref[pl.ds(d, chips, stride=CORES), :half] = part[:, d * half : (d + 1) * half]
            onehot = onehot_rows(sends_ref[line : line + 1, :], rows)
            total = total + pick_left(onehot, grads_ref[:, :half])
        full_ref[device] = pick_right(total, spread)
    own_conv_ref[...] = convs_ref[core]
    own_grad_ref[...] = full_ref[core]
    other_ref[:rows, :] = convs_ref[1 - core]
    other_ref[rows:, :] = full_ref[1 - core]


VMEM = pl.BlockSpec(memory_space=pltpu.VMEM)
HBM = pl.BlockSpec(memory_space=pl.ANY)
SMEM = pl.BlockSpec(memory_space=pltpu.SMEM)


def params(mebibytes):
    return pltpu.CompilerParams(vmem_limit_bytes=mebibytes * 1024 * 1024)


def whole(kernel, outs, args, in_specs=None, out_specs=None, scratch=(), mebibytes=16):
    return pl.pallas_call(
        kernel,
        out_shape=tuple(jax.ShapeDtypeStruct(s, t) for s, t in outs),
        in_specs=in_specs or [VMEM] * len(args),
        out_specs=tuple(out_specs or [VMEM] * len(outs)),
        scratch_shapes=list(scratch),
        compiler_params=params(mebibytes),
    )(*args)


def on_device(features, weights, cotangent, rule_src, rule_dst, block_count, send_rows):
    space = lax.axis_size("space")
    chan = lax.axis_size("chan")
    nz = space // (NY * CORES)
    rows, width = features.shape
    offsets = weights.shape[0]
    peers, slots = send_rows.shape
    halo_rows = peers * slots
    table_rows = rows + halo_rows
    half = width // CORES

    def place(y, z, core):
        return ((y % NY) * nz + z) * CORES + core

    where = [(y, z, core) for y in range(NY) for z in range(nz) for core in range(CORES)]
    z_groups = [[place(b, z, c) for z in range(nz)] for b in range(NY) for c in range(CORES)]
    core_groups = [[place(b, z, c) for b in range(NY) for z in range(nz)] for c in range(CORES)]
    chip_groups = [[place(b, z, c) for c in range(CORES)] for b in range(NY) for z in range(nz)]

    def along_y(x, step):
        return lax.ppermute(x, "space", [(place(y, z, c), place(y - step, z, c)) for y, z, c in where])

    def along_x(x, step):
        return lax.ppermute(x, "chan", [(a, (a - step) % chan) for a in range(chan)])

    def of_chip(x):
        return lax.all_gather(x, "space", axis=0, tiled=False, axis_index_groups=chip_groups)

    swapped = lax.ppermute(
        weights,
        ("space", "chan"),
        [(place(b, z, c) * chan + a, place(a, z, c) * chan + b) for b, z, c in where for a in range(chan)],
    )
    (shared,) = whole(
        prepare_kernel,
        [((SHARED, width), F32)],
        (block_count, features, cotangent, send_rows.T, rule_src, rule_dst),
        in_specs=[SMEM] + [HBM] * 5,
        scratch=[
            pltpu.VMEM((rows, width), F32),
            pltpu.VMEM((slots, peers), jnp.int32),
            pltpu.VMEM(rule_src.shape, jnp.int32),
            pltpu.VMEM(rule_dst.shape, jnp.int32),
            pltpu.SemaphoreType.DMA((5,)),
        ],
        mebibytes=LARGE,
    )
    shared = of_chip(shared).reshape(CORES * SHARED, width)
    swapped, shared = lax.optimization_barrier((swapped, shared))
    gathered = lax.all_gather(swapped, "space", axis=0, tiled=True, axis_index_groups=z_groups)
    (own,) = whole(regroup_kernel, [((offsets, 4 * nz, width), F32)], (gathered,), mebibytes=SMALL)
    shared, own = lax.optimization_barrier((shared, own))
    pieces = [own] + [along_y(own, s) for s in (1, 2, 3)]
    outgoing, cots, sends = whole(
        outgoing_kernel,
        [((halo_rows, width), F32), ((CORES * rows, width), F32), ((CORES * slots, peers), F32)],
        (shared,),
        scratch=[pltpu.VMEM((peers, width), F32)],
        mebibytes=SMALL,
    )
    cots = lax.all_gather(cots, "chan", axis=0, tiled=False)

    def exchange(x):
        x = x.reshape(peers // CORES, CORES * slots, width)
        x = lax.all_to_all(
            x, "space", split_axis=0, concat_axis=0, tiled=True, axis_index_groups=core_groups
        )
        return x.reshape(halo_rows, width)

    incoming = exchange(outgoing)
    halo_grad, local_grad, *parts = whole(
        core_kernel,
        [((halo_rows, width), F32), ((rows, width), F32)] + [((CORES * rows, width), F32)] * NY,
        (shared, incoming, cots, *pieces),
        in_specs=[HBM] * (NY + 3),
        out_specs=[HBM, VMEM] + [HBM] * NY,
        scratch=[
            pltpu.VMEM(shared.shape, F32),
            pltpu.VMEM(incoming.shape, F32),
            pltpu.VMEM((NY, CORES * rows, width), F32),
            pltpu.VMEM((NY, *own.shape), F32),
            pltpu.VMEM((NY * width, 2 * CORES * rows), BF16),
            pltpu.VMEM((CORES * table_rows, 2 * width), BF16),
            pltpu.VMEM((NY, CORES * rows, width), F32),
            pltpu.VMEM((halo_rows, width), F32),
            pltpu.SemaphoreType.DMA((2,)),
            pltpu.SemaphoreType.DMA((NY,)),
            pltpu.SemaphoreType.DMA((CHUNKS, NY)),
            pltpu.SemaphoreType.DMA((NY + 1,)),
        ],
        mebibytes=LARGE,
    )
    returned = exchange(halo_grad)
    parts = [parts[0]] + [along_x(parts[NY - s], s) for s in (2, 1, 3)]
    own_conv, own_grad, other = whole(
        finish_kernel,
        [((rows, width), F32)] * 2 + [((CORES * rows, width), F32)],
        (local_grad, returned, sends, *parts),
        scratch=[
            pltpu.VMEM((peers, width), F32),
            pltpu.VMEM((CORES, rows, width), F32),
            pltpu.VMEM((CORES, rows, width), F32),
        ],
        mebibytes=SMALL,
    )
    core = lax.axis_index("space") % CORES
    other = lax.dynamic_index_in_dim(of_chip(other), 1 - core, 0, False)
    return (own_conv + other[:rows], own_grad + other[rows:])


def solution(mesh):
    placed = (
        P("space", "chan"),
        P(None, "space", "chan"),
        P("space", "chan"),
        P("space", None),
        P("space", None),
        P("space"),
        P("space", None),
    )
    return jax.shard_map(
        on_device,
        mesh=mesh,
        in_specs=placed,
        out_specs=(P("space", "chan"), P("space", "chan")),
        check_vma=False,
    )
```

```python
import jax
import jax.numpy as jnp
from jax import lax
from jax.experimental import pallas as pl
from jax.experimental.pallas import tpu as pltpu
from jax.sharding import PartitionSpec as P

F32 = jnp.float32
BF16 = jnp.bfloat16
NY = 4
CORES = 2
SPANS = ((0, 6), (6, 27))
CHUNKS = len(SPANS)
SMALL, LARGE = 16, 63


def iota(shape, dim):
    return lax.broadcasted_iota(jnp.int32, shape, dim)


def split2(x):
    high = x.astype(BF16)
    return high, (x - high.astype(F32)).astype(BF16)


def dot(a, b):
    return jnp.dot(a, b, preferred_element_type=F32)


def chip_x():
    return lax.axis_index("chan")


def chip_y():
    return lax.axis_index("space") // (lax.axis_size("space") // NY)


def core_index():
    return lax.axis_index("space") % CORES


def as_onehot(mask):
    return jnp.where(mask, 1.0, 0.0).astype(BF16)


def pick_left(onehot, x):
    high, low = split2(x)
    return dot(onehot, high) + dot(onehot, low)


def pick_right(x, onehot):
    high, low = split2(x)
    return dot(high, onehot) + dot(low, onehot)


def to_inner(n):
    row = iota((n, n), 0)
    place = ((row >> 2) & 1) * 64 + (row >> 3) * 4 + (row & 3)
    return as_onehot(iota((n, n), 1) == place)


def from_inner(n):
    row = iota((n, n), 0)
    place = ((row >> 2) & 15) * 8 + (row >> 6) * 4 + (row & 3)
    return as_onehot(iota((n, n), 1) == place)


FEATURES, SOURCES, TARGETS, SENDS, SHARED = 128, 256, 288, 320, 328


def onehot_rows(line, rows):
    return as_onehot(line.astype(jnp.int32) == iota((rows, line.shape[1]), 0))


def started(pairs, sems):
    copies = [pltpu.make_async_copy(a, b, sems.at[i]) for i, (a, b) in enumerate(pairs)]
    for copy in copies:
        copy.start()
    return copies


def prepare_kernel(
    count_ref, features_in, cot_in, send_in, src_in, dst_in, shared_ref,
    features_ref, send_ref, src_ref, dst_ref, sems,
):
    rows, width = features_ref.shape
    offsets, block = src_ref.shape
    copies = started(
        [
            (features_in, features_ref),
            (send_in, send_ref),
            (src_in, src_ref),
            (dst_in, dst_ref),
            (cot_in, shared_ref.at[pl.ds(0, rows)]),
        ],
        sems,
    )
    for copy in copies:
        copy.wait()
    shared_ref[FEATURES : FEATURES + rows, :] = pick_right(features_ref[...], to_inner(width))
    shared_ref[SOURCES:SHARED, :] = jnp.zeros((SHARED - SOURCES, width), F32)
    for k in range(offsets):
        live = iota((1, block), 1) < count_ref[k]
        shared_ref[SOURCES + k : SOURCES + k + 1, :] = jnp.where(live, src_ref[k : k + 1, :], -1).astype(F32)
    shared_ref[TARGETS : TARGETS + offsets, :] = dst_ref[...].astype(F32)
    shared_ref[SENDS : SENDS + send_ref.shape[0], :] = send_ref[...].astype(F32)


def outgoing_kernel(shared_ref, outgoing_ref, cot_ref, sends_ref, picked_ref):
    rows, width = picked_ref.shape
    half = width // CORES
    slots = sends_ref.shape[0] // CORES
    chips = picked_ref.shape[0] // CORES
    for device in range(CORES):
        base = device * SHARED
        cot_ref[device * rows : (device + 1) * rows, :] = shared_ref[base : base + rows, :]
        inner = shared_ref[base + FEATURES : base + FEATURES + rows, :]
        parts = split2(pltpu.roll(inner, half * core_index(), axis=1))
        for slot in range(slots):
            line = shared_ref[base + SENDS + slot : base + SENDS + slot + 1, :]
            sends_ref[device * slots + slot : device * slots + slot + 1, :] = line
            onehot = onehot_rows(line, rows)
            high, low = (
                lax.dot_general(onehot, part, (((0,), (0,)), ((), ())), preferred_element_type=F32)
                for part in parts
            )
            picked_ref[...] = high + low
            both = [picked_ref[pl.ds(d, chips, stride=CORES), :][:, :half] for d in range(CORES)]
            outgoing_ref[pl.ds(device * slots + slot, chips, stride=CORES * slots), :] = jnp.concatenate(
                both, axis=1
            )


def regroup_kernel(gathered_ref, grouped_ref):
    offsets, inner, _ = grouped_ref.shape
    depth = gathered_ref.shape[1]
    for k in range(offsets):
        for z in range(inner // depth):
            grouped_ref[k, z * depth : (z + 1) * depth, :] = gathered_ref[z * offsets + k]


def pairs_of(shared_ref, device, k, local, rows):
    start = device * SHARED + k
    src = shared_ref[start + SOURCES : start + SOURCES + 1, :]
    dst = shared_ref[start + TARGETS : start + TARGETS + 1, :]
    mine = dst == iota((local, dst.shape[1]), 0).astype(F32)
    source = jnp.sum(jnp.where(mine, src + 1.0, 0.0), axis=1, keepdims=True)
    return as_onehot(iota((local, rows), 1) == source.astype(jnp.int32) - 1)


def kernel_rows(pieces):
    wide = jnp.concatenate(pieces, axis=2)
    return wide.reshape(wide.shape[0] * wide.shape[1], wide.shape[2])


def core_kernel(*refs):
    shared_in, incoming_in = refs[:2]
    cot_in = refs[2]
    piece_in = refs[3 : NY + 3]
    refs = refs[NY + 3 :]
    halo_out, local_ref, *part_outs = refs[: NY + 2]
    shared_ref, incoming_ref, cot_ref, pieces_ref, turned_ref, table_ref, total_ref, halo_ref = refs[
        NY + 2 : -4
    ]
    first_sems, cot_sems, piece_sems, out_sems = refs[-4:]
    both_rows, width = part_outs[0].shape
    rows = both_rows // CORES
    table_rows = table_ref.shape[0] // CORES
    half = pieces_ref.shape[2]
    x, y, core = chip_x(), chip_y(), core_index()

    def piece_copy(chunk, n):
        span = pl.ds(SPANS[chunk][0], SPANS[chunk][1] - SPANS[chunk][0])
        return pltpu.make_async_copy(piece_in[n].at[span], pieces_ref.at[n, span], piece_sems.at[chunk, n])

    shared_copy = pltpu.make_async_copy(shared_in, shared_ref, first_sems.at[0])
    incoming_copy = pltpu.make_async_copy(incoming_in, incoming_ref, first_sems.at[1])
    cots = [
        pltpu.make_async_copy(cot_in.at[(y + n) % NY], cot_ref.at[n], cot_sems.at[n]) for n in range(NY)
    ]
    for copy in [shared_copy, incoming_copy] + cots:
        copy.start()
    def pairs_at(chunk):
        return [
            jnp.concatenate(
                [pairs_of(shared_ref, d, k, rows, table_rows) for k in range(*SPANS[chunk])], axis=0
            )
            for d in range(CORES)
        ]

    shared_copy.wait()
    for chunk in range(CHUNKS):
        for n in range(NY):
            piece_copy(chunk, n).start()
    local = [
        pltpu.roll(
            shared_ref[d * SHARED + FEATURES : d * SHARED + FEATURES + rows, :], half * core, axis=1
        )[:, :half]
        for d in range(CORES)
    ]
    incoming_copy.wait()
    table = jnp.concatenate([jnp.concatenate(local, axis=1), incoming_ref[...]], axis=0)
    high, low = split2(table)
    table_ref[...] = jnp.zeros_like(table_ref)
    for d in range(CORES):
        mine = slice(d * half, (d + 1) * half)
        table_ref[d * table_rows : (d + 1) * table_rows, d * width : (d + 1) * width] = jnp.concatenate(
            [high[:, mine], low[:, mine]], axis=1
        )
    for copy in cots:
        copy.wait()
    for n in range(NY):
        high, low = split2(cot_ref[n].T)
        turned_ref[n * width : (n + 1) * width, :both_rows] = high
        turned_ref[n * width : (n + 1) * width, both_rows:] = low

    grads = [None] * CORES
    total = None
    for chunk in range(CHUNKS):
        step = SPANS[chunk][1] - SPANS[chunk][0]
        pairs = pairs_at(chunk)
        both = dot(jnp.concatenate(pairs, axis=1), table_ref[...]).astype(BF16)
        wide = [
            jnp.concatenate(
                [both[k * rows : (k + 1) * rows, d * width : (d + 1) * width] for k in range(step)], axis=1
            )
            for d in range(CORES)
        ]
        wide = jnp.concatenate(wide, axis=0)
        for n in range(NY):
            piece_copy(chunk, n).wait()
        span = slice(*SPANS[chunk])
        high, low = split2(kernel_rows([pieces_ref[n, span] for n in range(NY)]))

        def doubled(x):
            x = x.reshape(step, half, x.shape[1])
            return jnp.concatenate([x, x], axis=1).reshape(step * width, x.shape[2])

        highs = jnp.concatenate([wide[:, k * width : k * width + half] for k in range(step)], axis=1)
        product = dot(wide, doubled(high)) + dot(highs, low)
        total = product if chunk == 0 else total + product
        if chunk == CHUNKS - 1:
            outs = []
            for n in range(NY):
                total_ref[n] = total[:, n * width : (n + 1) * width]
            for s in range(NY):
                outs.append(
                    pltpu.make_async_copy(total_ref.at[(x + s - y + NY) % NY], part_outs[s], out_sems.at[s])
                )
                outs[-1].start()
        turned = dot(high, turned_ref[...])
        product = turned[:, :both_rows] + turned[:, both_rows:] + dot(low, turned_ref[:, :both_rows])
        product = product.reshape(step, half, both_rows)
        for device in range(CORES):
            side = jnp.concatenate(
                [product[k][:, device * rows : (device + 1) * rows] for k in range(step)], axis=1
            )
            both = dot(jnp.concatenate(split2(side), axis=0), pairs[device])
            both = both[:half] + both[half:]
            grads[device] = both if chunk == 0 else grads[device] + both
    table = jnp.concatenate(grads, axis=0).T
    halo_ref[...] = table[rows:, :]
    outs.append(pltpu.make_async_copy(halo_ref, halo_out, out_sems.at[NY]))
    outs[-1].start()
    local_ref[...] = table[:rows, :]
    for copy in outs:
        copy.wait()


def finish_kernel(local_ref, returned_ref, sends_ref, *refs):
    part_refs = refs[:NY]
    own_conv_ref, own_grad_ref, other_ref, grads_ref, convs_ref, full_ref = refs[NY:]
    rows, width = own_grad_ref.shape
    half = width // CORES
    slots = sends_ref.shape[0] // CORES
    chips = sends_ref.shape[1] // CORES
    core = core_index()
    conv = (part_refs[0][...] + part_refs[1][...]) + (part_refs[2][...] + part_refs[3][...])
    spread = from_inner(width)
    spread = jnp.where(core == 0, spread[:half, :], spread[half:, :])
    for device in range(CORES):
        convs_ref[device] = conv[device * rows : (device + 1) * rows, :]
        total = local_ref[:, device * half : (device + 1) * half]
        for slot in range(slots):
            line = device * slots + slot
            part = returned_ref[pl.ds(line, chips, stride=CORES * slots), :]
            for d in range(CORES):
                grads_ref[pl.ds(d, chips, stride=CORES), :half] = part[:, d * half : (d + 1) * half]
            onehot = onehot_rows(sends_ref[line : line + 1, :], rows)
            total = total + pick_left(onehot, grads_ref[:, :half])
        full_ref[device] = pick_right(total, spread)
    own_conv_ref[...] = convs_ref[core]
    own_grad_ref[...] = full_ref[core]
    other_ref[:rows, :] = convs_ref[1 - core]
    other_ref[rows:, :] = full_ref[1 - core]


VMEM = pl.BlockSpec(memory_space=pltpu.VMEM)
HBM = pl.BlockSpec(memory_space=pl.ANY)
SMEM = pl.BlockSpec(memory_space=pltpu.SMEM)


def params(mebibytes):
    return pltpu.CompilerParams(vmem_limit_bytes=mebibytes * 1024 * 1024)


def whole(kernel, outs, args, in_specs=None, out_specs=None, scratch=(), mebibytes=16):
    return pl.pallas_call(
        kernel,
        out_shape=tuple(jax.ShapeDtypeStruct(s, t) for s, t in outs),
        in_specs=in_specs or [VMEM] * len(args),
        out_specs=tuple(out_specs or [VMEM] * len(outs)),
        scratch_shapes=list(scratch),
        compiler_params=params(mebibytes),
    )(*args)


def on_device(features, weights, cotangent, rule_src, rule_dst, block_count, send_rows):
    space = lax.axis_size("space")
    chan = lax.axis_size("chan")
    nz = space // (NY * CORES)
    rows, width = features.shape
    offsets = weights.shape[0]
    peers, slots = send_rows.shape
    halo_rows = peers * slots
    table_rows = rows + halo_rows
    half = width // CORES

    def place(y, z, core):
        return ((y % NY) * nz + z) * CORES + core

    where = [(y, z, core) for y in range(NY) for z in range(nz) for core in range(CORES)]
    z_groups = [[place(b, z, c) for z in range(nz)] for b in range(NY) for c in range(CORES)]
    core_groups = [[place(b, z, c) for b in range(NY) for z in range(nz)] for c in range(CORES)]
    chip_groups = [[place(b, z, c) for c in range(CORES)] for b in range(NY) for z in range(nz)]

    def along_y(x, step):
        return lax.ppermute(x, "space", [(place(y, z, c), place(y - step, z, c)) for y, z, c in where])

    def along_x(x, step):
        return lax.ppermute(x, "chan", [(a, (a - step) % chan) for a in range(chan)])

    def of_chip(x):
        return lax.all_gather(x, "space", axis=0, tiled=False, axis_index_groups=chip_groups)

    swapped = lax.ppermute(
        weights,
        ("space", "chan"),
        [(place(b, z, c) * chan + a, place(a, z, c) * chan + b) for b, z, c in where for a in range(chan)],
    )
    (shared,) = whole(
        prepare_kernel,
        [((SHARED, width), F32)],
        (block_count, features, cotangent, send_rows.T, rule_src, rule_dst),
        in_specs=[SMEM] + [HBM] * 5,
        scratch=[
            pltpu.VMEM((rows, width), F32),
            pltpu.VMEM((slots, peers), jnp.int32),
            pltpu.VMEM(rule_src.shape, jnp.int32),
            pltpu.VMEM(rule_dst.shape, jnp.int32),
            pltpu.SemaphoreType.DMA((5,)),
        ],
        mebibytes=LARGE,
    )
    shared = of_chip(shared).reshape(CORES * SHARED, width)
    swapped, shared = lax.optimization_barrier((swapped, shared))
    gathered = lax.all_gather(swapped, "space", axis=0, tiled=True, axis_index_groups=z_groups)
    (own,) = whole(regroup_kernel, [((offsets, 4 * nz, width), F32)], (gathered,), mebibytes=SMALL)
    shared, own = lax.optimization_barrier((shared, own))
    pieces = [own] + [along_y(own, s) for s in (1, 2, 3)]
    outgoing, cots, sends = whole(
        outgoing_kernel,
        [((halo_rows, width), F32), ((CORES * rows, width), F32), ((CORES * slots, peers), F32)],
        (shared,),
        scratch=[pltpu.VMEM((peers, width), F32)],
        mebibytes=SMALL,
    )
    cots = lax.all_gather(cots, "chan", axis=0, tiled=False)

    def exchange(x):
        x = x.reshape(peers // CORES, CORES * slots, width)
        x = lax.all_to_all(
            x, "space", split_axis=0, concat_axis=0, tiled=True, axis_index_groups=core_groups
        )
        return x.reshape(halo_rows, width)

    incoming = exchange(outgoing)
    halo_grad, local_grad, *parts = whole(
        core_kernel,
        [((halo_rows, width), F32), ((rows, width), F32)] + [((CORES * rows, width), F32)] * NY,
        (shared, incoming, cots, *pieces),
        in_specs=[HBM] * (NY + 3),
        out_specs=[HBM, VMEM] + [HBM] * NY,
        scratch=[
            pltpu.VMEM(shared.shape, F32),
            pltpu.VMEM(incoming.shape, F32),
            pltpu.VMEM((NY, CORES * rows, width), F32),
            pltpu.VMEM((NY, *own.shape), F32),
            pltpu.VMEM((NY * width, 2 * CORES * rows), BF16),
            pltpu.VMEM((CORES * table_rows, 2 * width), BF16),
            pltpu.VMEM((NY, CORES * rows, width), F32),
            pltpu.VMEM((halo_rows, width), F32),
            pltpu.SemaphoreType.DMA((2,)),
            pltpu.SemaphoreType.DMA((NY,)),
            pltpu.SemaphoreType.DMA((CHUNKS, NY)),
            pltpu.SemaphoreType.DMA((NY + 1,)),
        ],
        mebibytes=LARGE,
    )
    returned = exchange(halo_grad)
    parts = [parts[0]] + [along_x(parts[NY - s], s) for s in (2, 1, 3)]
    own_conv, own_grad, other = whole(
        finish_kernel,
        [((rows, width), F32)] * 2 + [((CORES * rows, width), F32)],
        (local_grad, returned, sends, *parts),
        scratch=[
            pltpu.VMEM((peers, width), F32),
            pltpu.VMEM((CORES, rows, width), F32),
            pltpu.VMEM((CORES, rows, width), F32),
        ],
        mebibytes=SMALL,
    )
    core = lax.axis_index("space") % CORES
    other = lax.dynamic_index_in_dim(of_chip(other), 1 - core, 0, False)
    return (own_conv + other[:rows], own_grad + other[rows:])


def solution(mesh):
    placed = (
        P("space", "chan"),
        P(None, "space", "chan"),
        P("space", "chan"),
        P("space", None),
        P("space", None),
        P("space"),
        P("space", None),
    )
    return jax.shard_map(
        on_device,
        mesh=mesh,
        in_specs=placed,
        out_specs=(P("space", "chan"), P("space", "chan")),
        check_vma=False,
    )
```

```python
import jax
import jax.numpy as jnp
from jax import lax
from jax.experimental import pallas as pl
from jax.experimental.pallas import tpu as pltpu
from jax.sharding import PartitionSpec as P

F32 = jnp.float32
BF16 = jnp.bfloat16
NY = 4
CORES = 2
SPANS = ((0, 6), (6, 27))
CHUNKS = len(SPANS)
SMALL, LARGE = 16, 63


def iota(shape, dim):
    return lax.broadcasted_iota(jnp.int32, shape, dim)


def split2(x):
    high = x.astype(BF16)
    return high, (x - high.astype(F32)).astype(BF16)


def split3(x):
    high = x.astype(BF16)
    rest = x - high.astype(F32)
    middle = rest.astype(BF16)
    return high, middle, (rest - middle.astype(F32)).astype(BF16)


def dot(a, b):
    return jnp.dot(a, b, preferred_element_type=F32)


def chip_x():
    return lax.axis_index("chan")


def chip_y():
    return lax.axis_index("space") // (lax.axis_size("space") // NY)


def core_index():
    return lax.axis_index("space") % CORES


def as_onehot(mask):
    return jnp.where(mask, 1.0, 0.0).astype(BF16)


def pick_left(onehot, x):
    a, b, c = split3(x)
    return (dot(onehot, a) + dot(onehot, b)) + dot(onehot, c)


def pick_right(x, onehot):
    a, b, c = split3(x)
    return (dot(a, onehot) + dot(b, onehot)) + dot(c, onehot)


def to_inner(n):
    row = iota((n, n), 0)
    place = ((row >> 2) & 1) * 64 + (row >> 3) * 4 + (row & 3)
    return as_onehot(iota((n, n), 1) == place)


def from_inner(n):
    row = iota((n, n), 0)
    place = ((row >> 2) & 15) * 8 + (row >> 6) * 4 + (row & 3)
    return as_onehot(iota((n, n), 1) == place)


FEATURES, SOURCES, TARGETS, SENDS, SHARED = 128, 256, 288, 320, 328


def onehot_rows(line, rows):
    return as_onehot(line.astype(jnp.int32) == iota((rows, line.shape[1]), 0))


def started(pairs, sems):
    copies = [pltpu.make_async_copy(a, b, sems.at[i]) for i, (a, b) in enumerate(pairs)]
    for copy in copies:
        copy.start()
    return copies


def prepare_kernel(
    count_ref, features_in, cot_in, send_in, src_in, dst_in, shared_ref,
    features_ref, send_ref, src_ref, dst_ref, sems,
):
    rows, width = features_ref.shape
    offsets, block = src_ref.shape
    copies = started(
        [
            (features_in, features_ref),
            (send_in, send_ref),
            (src_in, src_ref),
            (dst_in, dst_ref),
            (cot_in, shared_ref.at[pl.ds(0, rows)]),
        ],
        sems,
    )
    for copy in copies:
        copy.wait()
    shared_ref[FEATURES : FEATURES + rows, :] = pick_right(features_ref[...], to_inner(width))
    shared_ref[SOURCES:SHARED, :] = jnp.zeros((SHARED - SOURCES, width), F32)
    for k in range(offsets):
        live = iota((1, block), 1) < count_ref[k]
        shared_ref[SOURCES + k : SOURCES + k + 1, :] = jnp.where(live, src_ref[k : k + 1, :], -1).astype(F32)
    shared_ref[TARGETS : TARGETS + offsets, :] = dst_ref[...].astype(F32)
    shared_ref[SENDS : SENDS + send_ref.shape[0], :] = send_ref[...].astype(F32)


def outgoing_kernel(shared_ref, outgoing_ref, cot_ref, sends_ref, picked_ref):
    rows, width = picked_ref.shape
    half = width // CORES
    slots = sends_ref.shape[0] // CORES
    chips = picked_ref.shape[0] // CORES
    for device in range(CORES):
        base = device * SHARED
        cot_ref[device * rows : (device + 1) * rows, :] = shared_ref[base : base + rows, :]
        inner = shared_ref[base + FEATURES : base + FEATURES + rows, :]
        parts = split3(pltpu.roll(inner, half * core_index(), axis=1))
        for slot in range(slots):
            line = shared_ref[base + SENDS + slot : base + SENDS + slot + 1, :]
            sends_ref[device * slots + slot : device * slots + slot + 1, :] = line
            onehot = onehot_rows(line, rows)
            a, b, c = (
                lax.dot_general(onehot, part, (((0,), (0,)), ((), ())), preferred_element_type=F32)
                for part in parts
            )
            picked_ref[...] = (a + b) + c
            both = [picked_ref[pl.ds(d, chips, stride=CORES), :][:, :half] for d in range(CORES)]
            outgoing_ref[pl.ds(device * slots + slot, chips, stride=CORES * slots), :] = jnp.concatenate(
                both, axis=1
            )


def regroup_kernel(gathered_ref, grouped_ref):
    offsets, inner, _ = grouped_ref.shape
    depth = gathered_ref.shape[1]
    for k in range(offsets):
        for z in range(inner // depth):
            grouped_ref[k, z * depth : (z + 1) * depth, :] = gathered_ref[z * offsets + k]


def pairs_of(shared_ref, device, k, local, rows):
    start = device * SHARED + k
    src = shared_ref[start + SOURCES : start + SOURCES + 1, :]
    dst = shared_ref[start + TARGETS : start + TARGETS + 1, :]
    mine = dst == iota((local, dst.shape[1]), 0).astype(F32)
    source = jnp.sum(jnp.where(mine, src + 1.0, 0.0), axis=1, keepdims=True)
    return as_onehot(iota((local, rows), 1) == source.astype(jnp.int32) - 1)


def kernel_rows(pieces):
    wide = jnp.concatenate(pieces, axis=2)
    return wide.reshape(wide.shape[0] * wide.shape[1], wide.shape[2])


def core_kernel(*refs):
    shared_in, incoming_in = refs[:2]
    cot_in = refs[2]
    piece_in = refs[3 : NY + 3]
    refs = refs[NY + 3 :]
    halo_out, local_ref, *part_outs = refs[: NY + 2]
    shared_ref, incoming_ref, cot_ref, pieces_ref, turned_ref, table_ref, total_ref, halo_ref = refs[
        NY + 2 : -4
    ]
    first_sems, cot_sems, piece_sems, out_sems = refs[-4:]
    both_rows, width = part_outs[0].shape
    rows = both_rows // CORES
    table_rows = table_ref.shape[0] // CORES
    half = pieces_ref.shape[2]
    x, y, core = chip_x(), chip_y(), core_index()

    def piece_copy(chunk, n):
        span = pl.ds(SPANS[chunk][0], SPANS[chunk][1] - SPANS[chunk][0])
        return pltpu.make_async_copy(piece_in[n].at[span], pieces_ref.at[n, span], piece_sems.at[chunk, n])

    shared_copy = pltpu.make_async_copy(shared_in, shared_ref, first_sems.at[0])
    incoming_copy = pltpu.make_async_copy(incoming_in, incoming_ref, first_sems.at[1])
    cots = [
        pltpu.make_async_copy(cot_in.at[(y + n) % NY], cot_ref.at[n], cot_sems.at[n]) for n in range(NY)
    ]
    for copy in [shared_copy, incoming_copy] + cots:
        copy.start()
    def pairs_at(chunk):
        return [
            jnp.concatenate(
                [pairs_of(shared_ref, d, k, rows, table_rows) for k in range(*SPANS[chunk])], axis=0
            )
            for d in range(CORES)
        ]

    shared_copy.wait()
    for chunk in range(CHUNKS):
        for n in range(NY):
            piece_copy(chunk, n).start()
    local = [
        pltpu.roll(
            shared_ref[d * SHARED + FEATURES : d * SHARED + FEATURES + rows, :], half * core, axis=1
        )[:, :half]
        for d in range(CORES)
    ]
    incoming_copy.wait()
    table = jnp.concatenate([jnp.concatenate(local, axis=1), incoming_ref[...]], axis=0)
    high, low = split2(table)
    table_ref[...] = jnp.zeros_like(table_ref)
    for d in range(CORES):
        mine = slice(d * half, (d + 1) * half)
        table_ref[d * table_rows : (d + 1) * table_rows, d * width : (d + 1) * width] = jnp.concatenate(
            [high[:, mine], low[:, mine]], axis=1
        )
    for copy in cots:
        copy.wait()
    for n in range(NY):
        high, low = split2(cot_ref[n].T)
        turned_ref[n * width : (n + 1) * width, :both_rows] = high
        turned_ref[n * width : (n + 1) * width, both_rows:] = low

    grads = [None] * CORES
    total = None
    for chunk in range(CHUNKS):
        step = SPANS[chunk][1] - SPANS[chunk][0]
        pairs = pairs_at(chunk)
        both = dot(jnp.concatenate(pairs, axis=1), table_ref[...]).astype(BF16)
        wide = [
            jnp.concatenate(
                [both[k * rows : (k + 1) * rows, d * width : (d + 1) * width] for k in range(step)], axis=1
            )
            for d in range(CORES)
        ]
        wide = jnp.concatenate(wide, axis=0)
        for n in range(NY):
            piece_copy(chunk, n).wait()
        span = slice(*SPANS[chunk])
        high, low = split2(kernel_rows([pieces_ref[n, span] for n in range(NY)]))

        def doubled(x):
            x = x.reshape(step, half, x.shape[1])
            return jnp.concatenate([x, x], axis=1).reshape(step * width, x.shape[2])

        highs = jnp.concatenate([wide[:, k * width : k * width + half] for k in range(step)], axis=1)
        product = dot(wide, doubled(high)) + dot(highs, low)
        total = product if chunk == 0 else total + product
        if chunk == CHUNKS - 1:
            outs = []
            for n in range(NY):
                total_ref[n] = total[:, n * width : (n + 1) * width]
            for s in range(NY):
                outs.append(
                    pltpu.make_async_copy(total_ref.at[(x + s - y + NY) % NY], part_outs[s], out_sems.at[s])
                )
                outs[-1].start()
        turned = dot(high, turned_ref[...])
        product = turned[:, :both_rows] + turned[:, both_rows:] + dot(low, turned_ref[:, :both_rows])
        product = product.reshape(step, half, both_rows)
        for device in range(CORES):
            side = jnp.concatenate(
                [product[k][:, device * rows : (device + 1) * rows] for k in range(step)], axis=1
            )
            both = dot(jnp.concatenate(split2(side), axis=0), pairs[device])
            both = both[:half] + both[half:]
            grads[device] = both if chunk == 0 else grads[device] + both
    table = jnp.concatenate(grads, axis=0).T
    halo_ref[...] = table[rows:, :]
    outs.append(pltpu.make_async_copy(halo_ref, halo_out, out_sems.at[NY]))
    outs[-1].start()
    local_ref[...] = table[:rows, :]
    for copy in outs:
        copy.wait()


def finish_kernel(local_ref, returned_ref, sends_ref, *refs):
    part_refs = refs[:NY]
    own_conv_ref, own_grad_ref, other_ref, grads_ref, convs_ref, full_ref = refs[NY:]
    rows, width = own_grad_ref.shape
    half = width // CORES
    slots = sends_ref.shape[0] // CORES
    chips = sends_ref.shape[1] // CORES
    core = core_index()
    conv = (part_refs[0][...] + part_refs[1][...]) + (part_refs[2][...] + part_refs[3][...])
    spread = from_inner(width)
    spread = jnp.where(core == 0, spread[:half, :], spread[half:, :])
    for device in range(CORES):
        convs_ref[device] = conv[device * rows : (device + 1) * rows, :]
        total = local_ref[:, device * half : (device + 1) * half]
        for slot in range(slots):
            line = device * slots + slot
            part = returned_ref[pl.ds(line, chips, stride=CORES * slots), :]
            for d in range(CORES):
                grads_ref[pl.ds(d, chips, stride=CORES), :half] = part[:, d * half : (d + 1) * half]
            onehot = onehot_rows(sends_ref[line : line + 1, :], rows)
            total = total + pick_left(onehot, grads_ref[:, :half])
        full_ref[device] = pick_right(total, spread)
    own_conv_ref[...] = convs_ref[core]
    own_grad_ref[...] = full_ref[core]
    other_ref[:rows, :] = convs_ref[1 - core]
    other_ref[rows:, :] = full_ref[1 - core]


VMEM = pl.BlockSpec(memory_space=pltpu.VMEM)
HBM = pl.BlockSpec(memory_space=pl.ANY)
SMEM = pl.BlockSpec(memory_space=pltpu.SMEM)


def params(mebibytes):
    return pltpu.CompilerParams(vmem_limit_bytes=mebibytes * 1024 * 1024)


def whole(kernel, outs, args, in_specs=None, out_specs=None, scratch=(), mebibytes=16):
    return pl.pallas_call(
        kernel,
        out_shape=tuple(jax.ShapeDtypeStruct(s, t) for s, t in outs),
        in_specs=in_specs or [VMEM] * len(args),
        out_specs=tuple(out_specs or [VMEM] * len(outs)),
        scratch_shapes=list(scratch),
        compiler_params=params(mebibytes),
    )(*args)


def on_device(features, weights, cotangent, rule_src, rule_dst, block_count, send_rows):
    space = lax.axis_size("space")
    chan = lax.axis_size("chan")
    nz = space // (NY * CORES)
    rows, width = features.shape
    offsets = weights.shape[0]
    peers, slots = send_rows.shape
    halo_rows = peers * slots
    table_rows = rows + halo_rows
    half = width // CORES

    def place(y, z, core):
        return ((y % NY) * nz + z) * CORES + core

    where = [(y, z, core) for y in range(NY) for z in range(nz) for core in range(CORES)]
    z_groups = [[place(b, z, c) for z in range(nz)] for b in range(NY) for c in range(CORES)]
    core_groups = [[place(b, z, c) for b in range(NY) for z in range(nz)] for c in range(CORES)]
    chip_groups = [[place(b, z, c) for c in range(CORES)] for b in range(NY) for z in range(nz)]

    def along_y(x, step):
        return lax.ppermute(x, "space", [(place(y, z, c), place(y - step, z, c)) for y, z, c in where])

    def along_x(x, step):
        return lax.ppermute(x, "chan", [(a, (a - step) % chan) for a in range(chan)])

    def of_chip(x):
        return lax.all_gather(x, "space", axis=0, tiled=False, axis_index_groups=chip_groups)

    swapped = lax.ppermute(
        weights,
        ("space", "chan"),
        [(place(b, z, c) * chan + a, place(a, z, c) * chan + b) for b, z, c in where for a in range(chan)],
    )
    (shared,) = whole(
        prepare_kernel,
        [((SHARED, width), F32)],
        (block_count, features, cotangent, send_rows.T, rule_src, rule_dst),
        in_specs=[SMEM] + [HBM] * 5,
        scratch=[
            pltpu.VMEM((rows, width), F32),
            pltpu.VMEM((slots, peers), jnp.int32),
            pltpu.VMEM(rule_src.shape, jnp.int32),
            pltpu.VMEM(rule_dst.shape, jnp.int32),
            pltpu.SemaphoreType.DMA((5,)),
        ],
        mebibytes=LARGE,
    )
    shared = of_chip(shared).reshape(CORES * SHARED, width)
    outgoing, cots, sends = whole(
        outgoing_kernel,
        [((halo_rows, width), F32), ((CORES * rows, width), F32), ((CORES * slots, peers), F32)],
        (shared,),
        scratch=[pltpu.VMEM((peers, width), F32)],
        mebibytes=SMALL,
    )
    swapped, shared, outgoing, cots = lax.optimization_barrier((swapped, shared, outgoing, cots))
    gathered = lax.all_gather(swapped, "space", axis=0, tiled=True, axis_index_groups=z_groups)
    (own,) = whole(regroup_kernel, [((offsets, 4 * nz, width), F32)], (gathered,), mebibytes=SMALL)
    shared, outgoing, cots, own = lax.optimization_barrier((shared, outgoing, cots, own))
    pieces = [own] + [along_y(own, s) for s in (1, 2, 3)]
    cots = lax.all_gather(cots, "chan", axis=0, tiled=False)

    def exchange(x):
        x = x.reshape(peers // CORES, CORES * slots, width)
        x = lax.all_to_all(
            x, "space", split_axis=0, concat_axis=0, tiled=True, axis_index_groups=core_groups
        )
        return x.reshape(halo_rows, width)

    incoming = exchange(outgoing)
    halo_grad, local_grad, *parts = whole(
        core_kernel,
        [((halo_rows, width), F32), ((rows, width), F32)] + [((CORES * rows, width), F32)] * NY,
        (shared, incoming, cots, *pieces),
        in_specs=[HBM] * (NY + 3),
        out_specs=[HBM, VMEM] + [HBM] * NY,
        scratch=[
            pltpu.VMEM(shared.shape, F32),
            pltpu.VMEM(incoming.shape, F32),
            pltpu.VMEM((NY, CORES * rows, width), F32),
            pltpu.VMEM((NY, *own.shape), F32),
            pltpu.VMEM((NY * width, 2 * CORES * rows), BF16),
            pltpu.VMEM((CORES * table_rows, 2 * width), BF16),
            pltpu.VMEM((NY, CORES * rows, width), F32),
            pltpu.VMEM((halo_rows, width), F32),
            pltpu.SemaphoreType.DMA((2,)),
            pltpu.SemaphoreType.DMA((NY,)),
            pltpu.SemaphoreType.DMA((CHUNKS, NY)),
            pltpu.SemaphoreType.DMA((NY + 1,)),
        ],
        mebibytes=LARGE,
    )
    returned = exchange(halo_grad)
    parts = [parts[0]] + [along_x(parts[NY - s], s) for s in (2, 1, 3)]
    own_conv, own_grad, other = whole(
        finish_kernel,
        [((rows, width), F32)] * 2 + [((CORES * rows, width), F32)],
        (local_grad, returned, sends, *parts),
        scratch=[
            pltpu.VMEM((peers, width), F32),
            pltpu.VMEM((CORES, rows, width), F32),
            pltpu.VMEM((CORES, rows, width), F32),
        ],
        mebibytes=SMALL,
    )
    core = lax.axis_index("space") % CORES
    other = lax.dynamic_index_in_dim(of_chip(other), 1 - core, 0, False)
    return (own_conv + other[:rows], own_grad + other[rows:])


def solution(mesh):
    placed = (
        P("space", "chan"),
        P(None, "space", "chan"),
        P("space", "chan"),
        P("space", None),
        P("space", None),
        P("space"),
        P("space", None),
    )
    return jax.shard_map(
        on_device,
        mesh=mesh,
        in_specs=placed,
        out_specs=(P("space", "chan"), P("space", "chan")),
        check_vma=False,
    )
```
